512 devices in a mesh: section: 4 (over z_hi), blk: 8 (over y), uly: 16 (over z_lo, x, core).
Axes of the slice: x: 4, y: 8, z: 8 (z_hi: 4, z_lo: 2; z = z_hi * 2 + z_lo), core: 2. Of those that a mesh axis runs over, the one named last changes fastest.
Arguments:
- stale: bfloat16 [4, 1280, 6144], P('section', ('blk', 'uly')), may hold values from -6 to 6
- layer_of_section: int32 [4], P('section'), may hold values from 0 to 15, as said below
- mod_table: float32 [16, 2, 6144], replicated, may hold values from -3 to 3
- w_qkv: bfloat16 [4, 6144, 48, 3, 128], P('section', 'blk', 'uly'), may hold values from -0.076546554 to 0.076546554
- q_gain: float32 [4, 48, 128], P('section', 'uly'), may hold values from 0.25 to 5.2
- k_gain: float32 [4, 48, 128], P('section', 'uly'), may hold values from 0.25 to 5.2
- counts: int32 [8], P('blk'), may hold values from 1 to 160, as said below
Outputs:
- mixed: bfloat16 [4, 1280, 6144], P('section', ('blk', 'uly'))
The draws below stay inside these ranges and needn't reach their ends.
Inputs may be any that keep to these rules, and one draw needn't show every extreme that they name: `layer_of_section`: each section runs a different layer; the first and the last layer are both run. `counts`: the valid tokens of a subgroup are its first ones; some subgroup is full.
All inputs are finite; a program needn't handle non-finite values.
Results may differ from the reference program's by a relative error of at most 0.029.
Values may be sent and summed in bfloat16 or wider, within the bound.
No kernel may reach another device: no remote copies, remote signals or barrier semaphores. Data moves between devices by JAX's collectives and lax.ppermute only.
A program may use at most 64 MiB of HBM per device.

```python
import jax
import jax.numpy as jnp
from jax import lax

D = 6144
HEADS = 48
HD = 128
LAYERS = 16
SECTIONS = 4
SUB_TOK = 160
TOKENS = 1280
N_BLK = 8


def gain_table(key, low, high):
    head_key, chan_key = jax.random.split(key)
    head = jnp.exp(jax.random.uniform(head_key, (SECTIONS, HEADS, 1), jnp.float32, jnp.log(low), jnp.log(high)))
    chan = jax.random.uniform(chan_key, (SECTIONS, HEADS, HD), jnp.float32, 0.85, 1.15)
    return head * chan


def draw_stale(key, part):
    key = jax.random.fold_in(key, 11)
    first = jax.random.fold_in(key, 0)
    base = jax.random.normal(first, (SECTIONS, TOKENS, D), jnp.float32)
    return jnp.clip(base, -6.0, 6.0).astype(jnp.bfloat16)


def draw_layer_of_section(key, part):
    key = jax.random.fold_in(key, 15)
    place_key, middle_key = jax.random.split(key)
    places = jax.random.permutation(place_key, jnp.arange(SECTIONS, dtype=jnp.int32))
    middle = 1 + jax.random.permutation(middle_key, jnp.arange(max(LAYERS - 2, 1), dtype=jnp.int32))
    ends = jnp.array([LAYERS - 1, 0], dtype=jnp.int32)
    values = jnp.concatenate([ends, middle.astype(jnp.int32)])[:SECTIONS]
    result = jnp.zeros((SECTIONS,), jnp.int32).at[places].set(values)
    return result.astype(jnp.int32)


def draw_counts(key, part):
    key = jax.random.fold_in(key, 16)
    pick_key, low_key, rest_key = jax.random.split(key, 3)
    full = jax.random.randint(pick_key, (), 0, N_BLK, dtype=jnp.int32)
    nextone = (full + 1) % N_BLK
    rest = jax.random.randint(rest_key, (N_BLK,), 1, SUB_TOK + 1, dtype=jnp.int32)
    short = jax.random.randint(low_key, (), 1, SUB_TOK // 2 + 1, dtype=jnp.int32)
    index = jnp.arange(N_BLK, dtype=jnp.int32)
    values = jnp.where(index == nextone, short, rest)
    values = jnp.where(index == full, jnp.int32(SUB_TOK), values)
    return values.astype(jnp.int32)


def draw_w_qkv(key, part):
    key = jax.random.fold_in(key, 12)
    base = jnp.clip(jax.random.normal(key, (SECTIONS, D, HEADS, 3, HD), jnp.float32), -6.0, 6.0) * D ** (-0.5)
    return base.astype(jnp.bfloat16)


def draw_q_gain(key, part):
    key = jax.random.fold_in(key, 13)
    return gain_table(key, 0.6, 2.0)


def draw_k_gain(key, part):
    key = jax.random.fold_in(key, 14)
    return gain_table(key, 0.6, 2.0)


def scatter_about(own_key, extent, scale, reach, kind=jnp.bfloat16):
    entries = jax.random.normal(own_key, extent, jnp.float32) * scale
    return jnp.minimum(jnp.maximum(entries, -reach), reach).astype(kind)


def setup_inputs(seed: int = 0) -> dict:
    keys = jax.random.split(jax.random.key(seed), 8)
    return {
        "stale": draw_stale(jax.random.fold_in(keys[7], 71), 0),
        "layer_of_section": draw_layer_of_section(jax.random.fold_in(keys[7], 71), 0),
        "mod_table": scatter_about(keys[2], (LAYERS, 2, D), 0.5, 3.0, jnp.float32),
        "w_qkv": draw_w_qkv(jax.random.fold_in(keys[7], 71), 0),
        "q_gain": draw_q_gain(jax.random.fold_in(keys[7], 71), 0),
        "k_gain": draw_k_gain(jax.random.fold_in(keys[7], 71), 0),
        "counts": draw_counts(jax.random.fold_in(keys[7], 71), 0),
    }


def head_norm(values, gain):
    scale = jnp.sqrt(lax.optimization_barrier(jnp.mean(values * values, axis=-1, keepdims=True)) + 1e-06)
    return values / scale * gain[None]

def reference(stale, layer_of_section, mod_table, w_qkv, q_gain, k_gain, counts):
    sections = stale.shape[0]
    width = D // N_BLK
    sub = TOKENS // N_BLK
    position = jnp.arange(TOKENS) % sub
    limit = jnp.repeat(counts, sub)
    valid = position < limit
    results = []
    for section_id in range(sections):
        source = stale[(section_id - 1) % sections].astype(jnp.float32)
        modul = mod_table[layer_of_section[section_id]]
        spread = jnp.sqrt(lax.optimization_barrier(jnp.mean(source * source, axis=-1, keepdims=True)) + 1e-06)
        normed = (source / spread * (1.0 + modul[1]) + modul[0]).astype(jnp.bfloat16)
        weights = w_qkv[section_id].reshape(D, HEADS * 3 * HD)
        total = jnp.zeros((TOKENS, HEADS * 3 * HD), jnp.float32)
        for index in range(N_BLK):
            product = jnp.dot(normed[:, index * width:(index + 1) * width], weights[index * width:(index + 1) * width], preferred_element_type=jnp.float32)
            total = total + lax.optimization_barrier(product.astype(jnp.bfloat16)).astype(jnp.float32)
        qkv = total.reshape(TOKENS, HEADS, 3, HD)
        query = head_norm(qkv[:, :, 0], q_gain[section_id]).astype(jnp.bfloat16)
        key_part = head_norm(qkv[:, :, 1], k_gain[section_id]).astype(jnp.bfloat16)
        value = qkv[:, :, 2].astype(jnp.bfloat16)
        scores = jnp.einsum('qhd,khd->hqk', query.astype(jnp.float32), key_part.astype(jnp.float32)) / jnp.sqrt(jnp.float32(HD))
        scores = jnp.where(valid[None, None, :], scores, -1e+30)
        top = lax.optimization_barrier(jnp.max(scores, axis=-1, keepdims=True))
        expo = jnp.exp(scores - top)
        denom = lax.optimization_barrier(jnp.sum(expo, axis=-1))
        probs = expo.astype(jnp.bfloat16)
        mixed = jnp.einsum('hqk,khd->qhd', probs.astype(jnp.float32), value.astype(jnp.float32))
        mixed = mixed / jnp.transpose(denom)[:, :, None]
        results.append(mixed.reshape(TOKENS, D).astype(jnp.bfloat16))
    return jnp.stack(results)
```

```python
import jax
import jax.numpy as jnp
from jax import lax
from jax.sharding import Mesh
from jax.sharding import PartitionSpec as P

AXES = ("section", "blk", "zlo", "x", "core")
CHIPS = ("zlo", "x")


def shifted(value, axis, steps):
    count = lax.axis_size(axis)
    pairs = [(source, (source + steps) % count) for source in range(count)]
    return lax.ppermute(value, axis, pairs)


def head_norm(values, gain):
    scale = jnp.sqrt(jnp.mean(values * values, axis=-1, keepdims=True) + 1e-06)
    return values / scale * gain


def on_device(stale, layer_of_section, mod_table, w_qkv, q_gain, k_gain, counts):
    tok_rows, width = stale.shape[1:]
    blks = lax.axis_size("blk")
    cores = lax.axis_size("core")
    chips = lax.axis_size("zlo") * lax.axis_size("x")
    slice_width, heads_dev = w_qkv.shape[1:3]
    head_size = w_qkv.shape[4]
    part = 3 * head_size
    heads_chip = cores * heads_dev
    sub_rows = tok_rows * chips * cores
    core = lax.axis_index("core")
    row = lax.axis_index("blk")

    weights = w_qkv[0].reshape(slice_width, heads_dev * part)
    weights = lax.all_gather(weights, "core", axis=0, tiled=False)
    gains = jnp.stack([q_gain[0], k_gain[0]])
    other = shifted(gains, "core", 1)
    gains = jnp.where(core == 0, jnp.stack([gains, other]), jnp.stack([other, gains]))
    owned = jnp.minimum(row, heads_chip - 1)
    gain = lax.dynamic_index_in_dim(
        gains.transpose(0, 2, 1, 3).reshape(heads_chip, 2, head_size), owned, 0, keepdims=False
    )

    received = shifted(stale[0], "section", 1)
    source = received.astype(jnp.float32)
    modul = lax.dynamic_index_in_dim(mod_table, layer_of_section[0], 0, keepdims=False)
    spread = jnp.sqrt(jnp.mean(source * source, axis=-1, keepdims=True) + 1e-06)
    normed = (source / spread * (1.0 + modul[1]) + modul[0]).astype(jnp.bfloat16)
    count_row = jnp.broadcast_to(counts.astype(jnp.bfloat16)[:, None], (6, width))
    sent = jnp.concatenate([normed, count_row], axis=0)
    sent = sent.reshape(sent.shape[0], blks, slice_width).transpose(1, 0, 2)
    sliced = lax.all_to_all(sent, "blk", 0, 0, tiled=False)
    all_counts = sliced[:, tok_rows, 0].astype(jnp.int32)
    mine = sliced[:, :tok_rows].reshape(blks * tok_rows, slice_width)
    copies = jnp.broadcast_to(mine[None], (chips,) + mine.shape)
    tokens = lax.all_to_all(copies, CHIPS, 0, 0, tiled=False)
    tokens = tokens.reshape(chips * blks * tok_rows, slice_width)
    rows = tokens.shape[0]

    products = []
    for index in range(cores):
        product = jnp.dot(tokens, weights[index], preferred_element_type=jnp.float32)
        product = product.astype(jnp.bfloat16).reshape(rows, heads_dev, part)
        products.append(product.transpose(1, 0, 2))
    products.append(jnp.zeros((blks - heads_chip, rows, part), jnp.bfloat16))
    products = jnp.concatenate(products, axis=0)
    qkv = lax.psum_scatter(products, "blk", scatter_dimension=0, tiled=False)
    qkv = qkv.astype(jnp.float32)
    query = head_norm(qkv[:, :head_size], gain[0]).astype(jnp.bfloat16)
    key_part = head_norm(qkv[:, head_size : 2 * head_size], gain[1]).astype(jnp.bfloat16)
    value = qkv[:, 2 * head_size :].astype(jnp.bfloat16)
    pair = jnp.concatenate([key_part, value], axis=1)
    pairs = jnp.concatenate([pair, shifted(pair, "core", 1)], axis=0)
    keys, values = pairs[:, :head_size], pairs[:, head_size:]

    lane = jnp.arange(cores)[:, None, None, None]
    lane = jnp.where(lane == 0, core, 1 - core)
    chip = jnp.arange(chips)[None, :, None, None]
    token = jnp.arange(tok_rows)[None, None, None, :]
    position = (chip * cores + lane) * tok_rows + token
    valid = (position < all_counts[None, None, :, None]).reshape(1, cores * rows)
    scores = jnp.dot(query, keys.T, preferred_element_type=jnp.float32) / jnp.sqrt(
        jnp.float32(head_size)
    )
    scores = jnp.where(valid, scores, -1e30)
    top = jnp.max(scores, axis=-1, keepdims=True)
    expo = jnp.exp(scores - top)
    denom = jnp.sum(expo, axis=-1, keepdims=True)
    mixed = jnp.dot(expo.astype(jnp.bfloat16), values, preferred_element_type=jnp.float32)
    mixed = (mixed / denom).astype(jnp.bfloat16)

    mixed = mixed.reshape(chips, blks, tok_rows, head_size).transpose(1, 0, 2, 3)
    mixed = mixed.reshape(blks * chips, tok_rows, head_size)
    returned = lax.all_to_all(mixed, ("blk",) + CHIPS, 0, 0, tiled=False)
    returned = returned.reshape(blks, chips, tok_rows, head_size)[:heads_chip]
    return returned.transpose(2, 1, 0, 3).reshape(1, tok_rows, width)


def solution(mesh):
    sizes = mesh.shape
    fine = Mesh(mesh.devices.reshape(sizes["section"], sizes["blk"], 2, 4, 2), AXES)
    uly = CHIPS + ("core",)
    in_specs = (
        P("section", ("blk",) + uly, None),
        P("section"),
        P(),
        P("section", "blk", uly, None, None),
        P("section", uly, None),
        P("section", uly, None),
        P("blk"),
    )
    out_specs = P("section", ("blk",) + uly, None)
    return jax.shard_map(
        on_device, mesh=fine, in_specs=in_specs, out_specs=out_specs, check_vma=False
    )
```

```python
import jax
import jax.numpy as jnp
from jax import lax
from jax.experimental import pallas as pl
from jax.experimental.pallas import tpu as pltpu
from jax.sharding import Mesh
from jax.sharding import PartitionSpec as P

AXES = ("section", "quad", "pair", "zlo", "x", "core")
ROWS = ("quad", "pair")
CHIPS = ("zlo", "x")


def swapped(value, axis):
    return lax.ppermute(value, axis, [(0, 1), (1, 0)])


def head_norm(values, gain):
    scale = jnp.sqrt(jnp.mean(values * values, axis=-1, keepdims=True) + 1e-06)
    return values / scale * gain


def product_kernel(tokens, held, other, out):
    heads, parts, depth, size = held.shape
    for head in range(heads):
        near = jnp.concatenate([held[head, part] for part in range(parts)], axis=1)
        far = jnp.concatenate([other[head, part] for part in range(parts)], axis=1)
        total = jnp.dot(tokens[:, :depth], near, preferred_element_type=jnp.float32)
        total += jnp.dot(tokens[:, depth:], far, preferred_element_type=jnp.float32)
        out[head] = total.astype(out.dtype)
    for head in range(heads, out.shape[0]):
        out[head] = jnp.zeros(out.shape[1:], out.dtype)


def products(tokens, held, other, blocks):
    heads, parts, depth, size = held.shape
    rows = tokens.shape[0]
    whole = pl.BlockSpec(memory_space=pltpu.VMEM)
    return pl.pallas_call(
        product_kernel,
        out_shape=jax.ShapeDtypeStruct((blocks, rows, parts * size), jnp.bfloat16),
        in_specs=[whole] * 3,
        out_specs=whole,
        compiler_params=pltpu.CompilerParams(vmem_limit_bytes=32 * 2**20),
        cost_estimate=pl.CostEstimate(
            flops=4 * rows * depth * heads * parts * size, bytes_accessed=8 * 2**20, transcendentals=0
        ),
    )(tokens, held, other)


def on_device(stale, layer_of_section, mod_table, w_qkv, q_gain, k_gain, counts):
    tok_rows, width = stale.shape[1:]
    quads = lax.axis_size("quad")
    pairs = lax.axis_size("pair")
    cores = lax.axis_size("core")
    chips = lax.axis_size("zlo") * lax.axis_size("x")
    slice_width, heads_dev = w_qkv.shape[1:3]
    head_size = w_qkv.shape[4]
    blks = quads * pairs
    core = lax.axis_index("core")
    pair = lax.axis_index("pair")
    quad = lax.axis_index("quad")
    same = core == pair

    received = lax.ppermute(stale[0], "section", [(i, (i + 1) % 4) for i in range(4)])

    weights = w_qkv[0].transpose(1, 2, 0, 3)
    moved = lax.ppermute(weights, ("pair", "core"), [(1, 2), (2, 1)])
    held = jnp.where(same, weights, moved)
    other = swapped(held, "core")
    gains = jnp.stack([q_gain[0], k_gain[0]])
    gains = jnp.where(same, gains, swapped(gains, "core"))
    owned = jnp.minimum(quad, heads_dev - 1)
    gain = lax.dynamic_index_in_dim(gains, owned, 1, keepdims=False)

    source = received.astype(jnp.float32)
    modul = lax.dynamic_index_in_dim(mod_table, layer_of_section[0], 0, keepdims=False)
    spread = jnp.sqrt(jnp.mean(source * source, axis=-1, keepdims=True) + 1e-06)
    normed = (source / spread * (1.0 + modul[1]) + modul[0]).astype(jnp.bfloat16)
    count_rows = jnp.broadcast_to(counts.astype(jnp.bfloat16)[:, None], (6, width))
    sent = jnp.concatenate([normed, count_rows], axis=0)
    sent = sent.reshape(sent.shape[0], quads, 2, slice_width)
    sent = jnp.where(core == 0, sent, sent[:, :, ::-1])
    sent = sent.reshape(sent.shape[0], quads, 1, 2 * slice_width).transpose(1, 2, 0, 3)
    sent = jnp.broadcast_to(sent, (quads, pairs) + sent.shape[2:])
    sent = sent.reshape((blks,) + sent.shape[2:])
    sliced = lax.all_to_all(sent, ROWS, 0, 0, tiled=False)
    all_counts = sliced[:, tok_rows, 0].astype(jnp.int32)
    mine = sliced[:, :tok_rows].reshape(blks * tok_rows, 2 * slice_width)
    copies = jnp.broadcast_to(mine[None], (chips,) + mine.shape)
    tokens = lax.all_to_all(copies, CHIPS, 0, 0, tiled=False)
    tokens = tokens.reshape(chips * blks * tok_rows, 2 * slice_width)
    rows = tokens.shape[0]

    partial = products(tokens, held, other, quads)
    partial = lax.all_to_all(partial, "quad", 0, 0, tiled=False)
    qkv = jnp.sum(partial.astype(jnp.float32), axis=0)
    query = head_norm(qkv[:, :head_size], gain[0]).astype(jnp.bfloat16)
    key_part = head_norm(qkv[:, head_size : 2 * head_size], gain[1]).astype(jnp.bfloat16)
    value = qkv[:, 2 * head_size :].astype(jnp.bfloat16)
    near = jnp.concatenate([key_part, value], axis=1)
    both = jnp.concatenate([near, swapped(near, "core")], axis=0)
    keys, values = both[:, :head_size], both[:, head_size:]

    lane = jnp.arange(cores)[:, None, None, None]
    lane = jnp.where(lane == 0, core, 1 - core)
    chip = jnp.arange(chips)[None, :, None, None]
    token = jnp.arange(tok_rows)[None, None, None, :]
    position = (chip * cores + lane) * tok_rows + token
    valid = (position < all_counts[None, None, :, None]).reshape(1, cores * rows)
    scores = jnp.dot(query, keys.T, preferred_element_type=jnp.float32) / jnp.sqrt(
        jnp.float32(head_size)
    )
    scores = jnp.where(valid, scores, -1e30)
    top = jnp.max(scores, axis=-1, keepdims=True)
    expo = jnp.exp(scores - top)
    denom = jnp.sum(expo, axis=-1, keepdims=True)
    mixed = jnp.dot(expo.astype(jnp.bfloat16), values, preferred_element_type=jnp.float32)
    mixed = (mixed / denom).astype(jnp.bfloat16)

    mixed = mixed.reshape(chips, blks, tok_rows, head_size).transpose(1, 0, 2, 3)
    mixed = mixed.reshape(blks * chips, tok_rows, head_size)
    returned = lax.all_to_all(mixed, ROWS + CHIPS, 0, 0, tiled=False)
    returned = returned.reshape(quads, pairs, chips, tok_rows, head_size)[:heads_dev]
    return returned.transpose(3, 2, 1, 0, 4).reshape(1, tok_rows, width)


def solution(mesh):
    sizes = mesh.shape
    fine = Mesh(mesh.devices.reshape(sizes["section"], 4, 2, 2, 4, 2), AXES)
    uly = CHIPS + ("core",)
    in_specs = (
        P("section", ROWS + uly, None),
        P("section"),
        P(),
        P("section", ROWS, uly, None, None),
        P("section", uly, None),
        P("section", uly, None),
        P(ROWS),
    )
    out_specs = P("section", ROWS + uly, None)
    return jax.shard_map(
        on_device, mesh=fine, in_specs=in_specs, out_specs=out_specs, check_vma=False
    )
```

```python
import jax
import jax.numpy as jnp
from jax import lax
from jax.experimental import pallas as pl
from jax.experimental.pallas import tpu as pltpu
from jax.sharding import Mesh
from jax.sharding import PartitionSpec as P

AXES = ("section", "blk", "zlo", "x", "core")
CHIPS = ("zlo", "x")
SMALL = pl.BlockSpec(memory_space=pltpu.SMEM)
WHOLE = pl.BlockSpec(memory_space=pltpu.VMEM)
DISTANT = pl.BlockSpec(memory_space=pltpu.HBM)
LIMIT = pltpu.CompilerParams(vmem_limit_bytes=12 * 2**20)


def shifted(value, axis, steps):
    count = lax.axis_size(axis)
    pairs = [(source, (source + steps) % count) for source in range(count)]
    return lax.ppermute(value, axis, pairs)


def head_norm(values, gain):
    scale = jnp.sqrt(jnp.mean(values * values, axis=-1, keepdims=True) + 1e-06)
    return values / scale * gain


def pack_kernel(counts, stale, modul, out):
    rows, width = stale.shape
    blks, padded, slice_width = out.shape
    source = stale[...].astype(jnp.float32)
    spread = jnp.sqrt(jnp.mean(source * source, axis=-1, keepdims=True) + 1e-06)
    normed = source / spread * (1.0 + modul[1:2]) + modul[0:1]
    count = jnp.full((padded - rows, width), counts[0], jnp.int32).astype(jnp.float32)
    normed = jnp.concatenate([normed, count], axis=0).astype(out.dtype)
    for blk in range(blks):
        out[blk] = normed[:, blk * slice_width : (blk + 1) * slice_width]


def packed(counts, stale, modul, shape):
    return pl.pallas_call(
        pack_kernel,
        out_shape=jax.ShapeDtypeStruct(shape, jnp.bfloat16),
        in_specs=[SMALL, WHOLE, WHOLE],
        out_specs=WHOLE,
        compiler_params=LIMIT,
        cost_estimate=pl.CostEstimate(flops=10**6, bytes_accessed=10**6, transcendentals=0),
    )(counts, stale, modul)


def product_kernel(steps, place, tokens, own, other, *refs):
    outs, block, sems = refs[: len(steps)], refs[-2], refs[-1]
    row, core = place[0], place[1]
    heads, parts = own.shape[:2]

    def fetch(number):
        owner = lax.rem(row + steps[number], lax.axis_size("blk"))
        head = jnp.minimum(owner, 2 * heads - 1)
        lane = jnp.where(head >= heads, 1, 0)
        slot = number % 2

        @pl.when(lane == core)
        def _():
            pltpu.make_async_copy(own.at[head - lane * heads], block.at[slot], sems.at[slot]).start()

        @pl.when(lane != core)
        def _():
            pltpu.make_async_copy(other.at[head - lane * heads], block.at[slot], sems.at[slot]).start()

    fetch(0)
    for number, out in enumerate(outs):
        slot = number % 2
        if number + 1 < len(outs):
            fetch(number + 1)
        pltpu.make_async_copy(own.at[0], block.at[slot], sems.at[slot]).wait()
        weights = jnp.concatenate([block[slot, part] for part in range(parts)], axis=1)
        total = jnp.dot(tokens[...], weights, preferred_element_type=jnp.float32)
        out[...] = total.astype(out.dtype)


def products(steps, place, tokens, own, other):
    rows, depth = tokens.shape
    parts, size = own.shape[1], own.shape[3]
    shape = jax.ShapeDtypeStruct((rows, parts * size), jnp.bfloat16)
    return pl.pallas_call(
        lambda *refs: product_kernel(steps, *refs),
        out_shape=[shape] * len(steps),
        in_specs=[SMALL, WHOLE, DISTANT, DISTANT],
        out_specs=[WHOLE] * len(steps),
        scratch_shapes=[
            pltpu.VMEM((2,) + own.shape[1:], jnp.bfloat16),
            pltpu.SemaphoreType.DMA((2,)),
        ],
        compiler_params=LIMIT,
        cost_estimate=pl.CostEstimate(
            flops=2 * rows * depth * parts * size * len(steps), bytes_accessed=4 * 2**20, transcendentals=0
        ),
    )(place, tokens, own, other)


def add_kernel(begin, first, second, out):
    rows = second.shape[0]
    total = first[begin : begin + rows].astype(jnp.float32) + second[...].astype(jnp.float32)
    out[begin : begin + rows] = total.astype(out.dtype)
    for low, high in ((0, begin), (begin + rows, out.shape[0])):
        if high > low:
            out[low:high] = first[low:high]


def added(first, second, begin=0):
    return pl.pallas_call(
        lambda *refs: add_kernel(begin, *refs),
        out_shape=jax.ShapeDtypeStruct(first.shape, first.dtype),
        in_specs=[WHOLE, WHOLE],
        out_specs=WHOLE,
        compiler_params=LIMIT,
        cost_estimate=pl.CostEstimate(flops=first.size, bytes_accessed=3 * 2**19, transcendentals=0),
    )(first, second)


def head_kernel(first, second, third, gain, query, pair):
    size = query.shape[1]
    total = first[...].astype(jnp.float32) + second[...].astype(jnp.float32)
    total = total + third[...].astype(jnp.float32)
    query[...] = head_norm(total[:, :size], gain[0:1]).astype(query.dtype)
    pair[:, :size] = head_norm(total[:, size : 2 * size], gain[1:2]).astype(pair.dtype)
    pair[:, size:] = total[:, 2 * size :].astype(pair.dtype)


def headed(first, second, third, gain):
    rows, size = first.shape[0], gain.shape[1]
    return pl.pallas_call(
        head_kernel,
        out_shape=[
            jax.ShapeDtypeStruct((rows, size), jnp.bfloat16),
            jax.ShapeDtypeStruct((rows, 2 * size), jnp.bfloat16),
        ],
        in_specs=[WHOLE] * 4,
        out_specs=[WHOLE] * 2,
        compiler_params=LIMIT,
        cost_estimate=pl.CostEstimate(flops=10 * first.size, bytes_accessed=4 * 2**19, transcendentals=0),
    )(first, second, third, gain)


def merge_kernel(blocks, out):
    blks, chips = blocks.shape[:2]
    size = blocks.shape[3]
    heads = out.shape[2] // (chips * size)
    for chip in range(chips):
        for blk in range(heads):
            begin = (chip * heads + blk) * size
            out[0, :, begin : begin + size] = blocks[blk, chip]


def merged(blocks, shape):
    return pl.pallas_call(
        merge_kernel,
        out_shape=jax.ShapeDtypeStruct(shape, blocks.dtype),
        in_specs=[WHOLE],
        out_specs=WHOLE,
        compiler_params=LIMIT,
        cost_estimate=pl.CostEstimate(flops=0, bytes_accessed=2**19, transcendentals=0),
    )(blocks)


def on_device(stale, layer_of_section, mod_table, w_qkv, q_gain, k_gain, counts):
    tok_rows, width = stale.shape[1:]
    blks = lax.axis_size("blk")
    cores = lax.axis_size("core")
    chips = lax.axis_size("zlo") * lax.axis_size("x")
    slice_width, heads_dev = w_qkv.shape[1:3]
    head_size = w_qkv.shape[4]
    heads_chip = cores * heads_dev
    core = lax.axis_index("core")
    row = lax.axis_index("blk")

    received = shifted(stale[0], "section", 1)
    modul = lax.dynamic_index_in_dim(mod_table, layer_of_section[0], 0, keepdims=False)
    own = w_qkv[0].transpose(1, 2, 0, 3)
    gains = jnp.concatenate([q_gain, k_gain], axis=0)
    other = shifted(own, "core", 1)
    theirs = shifted(gains, "core", 1)
    owned = jnp.minimum(row, heads_chip - 1)
    lane = owned // heads_dev
    gain = jnp.where(lane == core, gains, theirs)
    gain = lax.dynamic_index_in_dim(gain, owned - lane * heads_dev, 1, keepdims=False)

    sent = packed(counts, received, modul, (blks, 16, slice_width))
    sliced = lax.all_to_all(sent, "blk", 0, 0, tiled=False)
    all_counts = sliced[:, tok_rows, 0].astype(jnp.int32)
    mine = sliced[:, :tok_rows].reshape(blks * tok_rows, slice_width)
    copies = jnp.broadcast_to(mine[None], (chips,) + mine.shape)
    tokens = lax.all_to_all(copies, CHIPS, 0, 0, tiled=False)
    tokens = tokens.reshape(chips * blks * tok_rows, slice_width)
    rows = tokens.shape[0]
    half = rows // 2

    place = jnp.stack([row, core]).astype(jnp.int32)
    (far,) = products((4,), place, tokens, own, other)
    up, down = shifted(far[:half], "blk", 1), shifted(far[half:], "blk", -1)
    three, five = products((3, 5), place, tokens, own, other)
    up, down = shifted(added(three, up), "blk", 1), shifted(added(five, down, half), "blk", -1)
    two, six = products((2, 6), place, tokens, own, other)
    up, down = shifted(added(two, up), "blk", 1), shifted(added(six, down), "blk", -1)
    one, seven, zero = products((1, 7, 0), place, tokens, own, other)
    up, down = shifted(added(one, up), "blk", 1), shifted(added(seven, down), "blk", -1)
    query, near = headed(zero, up, down, gain)
    both = jnp.concatenate([near, shifted(near, "core", 1)], axis=0)
    keys, values = both[:, :head_size], both[:, head_size:]

    lane = jnp.arange(cores)[:, None, None, None]
    lane = jnp.where(lane == 0, core, 1 - core)
    chip = jnp.arange(chips)[None, :, None, None]
    token = jnp.arange(tok_rows)[None, None, None, :]
    position = (chip * cores + lane) * tok_rows + token
    valid = (position < all_counts[None, None, :, None]).reshape(1, cores * rows)
    scores = jnp.dot(query, keys.T, preferred_element_type=jnp.float32) / jnp.sqrt(
        jnp.float32(head_size)
    )
    scores = jnp.where(valid, scores, -1e30)
    top = jnp.max(scores, axis=-1, keepdims=True)
    expo = jnp.exp(scores - top)
    denom = jnp.sum(expo, axis=-1, keepdims=True)
    mixed = jnp.dot(expo.astype(jnp.bfloat16), values, preferred_element_type=jnp.float32)
    mixed = (mixed / denom).astype(jnp.bfloat16)

    mixed = mixed.reshape(chips, blks, tok_rows, head_size).transpose(1, 0, 2, 3)
    mixed = mixed.reshape(blks * chips, tok_rows, head_size)
    returned = lax.all_to_all(mixed, ("blk",) + CHIPS, 0, 0, tiled=False)
    return merged(returned.reshape(blks, chips, tok_rows, head_size), (1, tok_rows, width))


def solution(mesh):
    sizes = mesh.shape
    fine = Mesh(mesh.devices.reshape(sizes["section"], sizes["blk"], 2, 4, 2), AXES)
    uly = CHIPS + ("core",)
    in_specs = (
        P("section", ("blk",) + uly, None),
        P("section"),
        P(),
        P("section", "blk", uly, None, None),
        P("section", uly, None),
        P("section", uly, None),
        P("blk"),
    )
    out_specs = P("section", ("blk",) + uly, None)
    return jax.shard_map(
        on_device, mesh=fine, in_specs=in_specs, out_specs=out_specs, check_vma=False
    )
```

```python
import jax
import jax.numpy as jnp
from jax import lax
from jax.experimental import pallas as pl
from jax.experimental.pallas import tpu as pltpu
from jax.sharding import Mesh
from jax.sharding import PartitionSpec as P

AXES = ("section", "blk", "zlo", "x", "core")
CHIPS = ("zlo", "x")
SMALL = pl.BlockSpec(memory_space=pltpu.SMEM)
WHOLE = pl.BlockSpec(memory_space=pltpu.VMEM)
DISTANT = pl.BlockSpec(memory_space=pltpu.HBM)
LIMIT = pltpu.CompilerParams(vmem_limit_bytes=12 * 2**20)


def shifted(value, axis, steps):
    count = lax.axis_size(axis)
    pairs = [(source, (source + steps) % count) for source in range(count)]
    return lax.ppermute(value, axis, pairs)


def head_norm(values, gain):
    scale = jnp.sqrt(jnp.mean(values * values, axis=-1, keepdims=True) + 1e-06)
    return values / scale * gain


def stack_kernel(q_gain, k_gain, gains):
    heads = q_gain.shape[0]
    for head in range(heads):
        gains[head : head + 1] = q_gain[head]
        gains[heads + head : heads + head + 1] = k_gain[head]


def stacked(q_gain, k_gain):
    return pl.pallas_call(
        stack_kernel,
        out_shape=jax.ShapeDtypeStruct((2 * q_gain.shape[0], q_gain.shape[2]), jnp.float32),
        in_specs=[WHOLE, WHOLE],
        out_specs=WHOLE,
        compiler_params=LIMIT,
        cost_estimate=pl.CostEstimate(flops=0, bytes_accessed=2**14, transcendentals=0),
    )(q_gain, k_gain)


def pack_kernel(counts, place, stale, modul, out):
    rows, width = stale.shape
    blks, padded, slice_width = out.shape
    source = stale[...].astype(jnp.float32)
    spread = jnp.sqrt(jnp.mean(source * source, axis=-1, keepdims=True) + 1e-06)
    normed = source / spread * (1.0 + modul[1:2]) + modul[0:1]
    count = jnp.full((padded - rows, width), counts[0], jnp.int32).astype(jnp.float32)
    normed = jnp.concatenate([normed, count], axis=0).astype(out.dtype)
    for blk in range(blks):
        out[blk] = normed[:, blk * slice_width : (blk + 1) * slice_width]


def packed(counts, place, stale, modul, shape):
    return pl.pallas_call(
        pack_kernel,
        out_shape=jax.ShapeDtypeStruct(shape, jnp.bfloat16),
        in_specs=[SMALL, SMALL, WHOLE, WHOLE],
        out_specs=WHOLE,
        compiler_params=LIMIT,
        cost_estimate=pl.CostEstimate(flops=10**10, bytes_accessed=10**6, transcendentals=0),
    )(counts, place, stale, modul)


def spread_kernel(sliced, weights, out, rows):
    blks = sliced.shape[0]
    count = out.shape[1] // blks
    for blk in range(blks):
        rows[blk * count : (blk + 1) * count] = sliced[blk, :count].astype(jnp.float32)
    block = rows[...].astype(out.dtype)
    for chip in range(out.shape[0]):
        out[chip] = block


def spread(sliced, weights, shape):
    return pl.pallas_call(
        spread_kernel,
        out_shape=jax.ShapeDtypeStruct(shape, jnp.bfloat16),
        in_specs=[WHOLE, DISTANT],
        out_specs=WHOLE,
        scratch_shapes=[pltpu.VMEM(shape[1:], jnp.float32)],
        compiler_params=LIMIT,
        cost_estimate=pl.CostEstimate(flops=0, bytes_accessed=10**6, transcendentals=0),
    )(sliced, weights)


def product_kernel(steps, place, tokens, own, other, *refs):
    outs, block, sems = refs[:-2], refs[-2], refs[-1]
    pieces = len(outs) // len(steps)
    size = tokens.shape[0] // pieces
    row, core = place[0], place[1]
    heads, parts = own.shape[:2]

    def fetch(number):
        owner = lax.rem(row + steps[number], lax.axis_size("blk"))
        head = jnp.minimum(owner, 2 * heads - 1)
        lane = jnp.where(head >= heads, 1, 0)
        slot = number % 2

        @pl.when(lane == core)
        def _():
            pltpu.make_async_copy(own.at[head - lane * heads], block.at[slot], sems.at[slot]).start()

        @pl.when(lane != core)
        def _():
            pltpu.make_async_copy(other.at[head - lane * heads], block.at[slot], sems.at[slot]).start()

    fetch(0)
    for number in range(len(steps)):
        slot = number % 2
        if number + 1 < len(steps):
            fetch(number + 1)
        pltpu.make_async_copy(own.at[0], block.at[slot], sems.at[slot]).wait()
        weights = jnp.concatenate([block[slot, part] for part in range(parts)], axis=1)
        total = jnp.dot(tokens[...], weights, preferred_element_type=jnp.float32)
        for piece in range(pieces):
            out = outs[number * pieces + piece]
            out[...] = total[piece * size : (piece + 1) * size].astype(out.dtype)


def products(steps, place, tokens, own, other, pieces=1):
    rows, depth = tokens.shape
    parts, size = own.shape[1], own.shape[3]
    shape = jax.ShapeDtypeStruct((rows // pieces, parts * size), jnp.bfloat16)
    return pl.pallas_call(
        lambda *refs: product_kernel(steps, *refs),
        out_shape=[shape] * (pieces * len(steps)),
        in_specs=[SMALL, WHOLE, DISTANT, DISTANT],
        out_specs=[WHOLE] * (pieces * len(steps)),
        scratch_shapes=[
            pltpu.VMEM((2,) + own.shape[1:], jnp.bfloat16),
            pltpu.SemaphoreType.DMA((2,)),
        ],
        compiler_params=LIMIT,
        cost_estimate=pl.CostEstimate(
            flops=2 * rows * depth * parts * size * len(steps), bytes_accessed=4 * 2**20, transcendentals=0
        ),
    )(place, tokens, own, other)


def add_kernel(begin, first, second, out):
    rows = second.shape[0]
    total = first[begin : begin + rows].astype(jnp.float32) + second[...].astype(jnp.float32)
    out[begin : begin + rows] = total.astype(out.dtype)
    for low, high in ((0, begin), (begin + rows, out.shape[0])):
        if high > low:
            out[low:high] = first[low:high]


def added(first, second, begin=0):
    return pl.pallas_call(
        lambda *refs: add_kernel(begin, *refs),
        out_shape=jax.ShapeDtypeStruct(first.shape, first.dtype),
        in_specs=[WHOLE, WHOLE],
        out_specs=WHOLE,
        compiler_params=LIMIT,
        cost_estimate=pl.CostEstimate(flops=first.size, bytes_accessed=3 * 2**19, transcendentals=0),
    )(first, second)


def head_kernel(place, first, second, third, gains, theirs, query, pair):
    size = query.shape[1]
    heads = gains.shape[0] // 2
    owned = jnp.minimum(place[0], 2 * heads - 1)
    lane = jnp.where(owned >= heads, 1, 0)
    index = owned - lane * heads
    mine = lane == place[1]
    gain = []
    for part in range(2):
        at = pl.ds(part * heads + index, 1)
        gain.append(jnp.where(mine, gains[at], theirs[at]))
    total = first[...].astype(jnp.float32) + second[...].astype(jnp.float32)
    total = total + third[...].astype(jnp.float32)
    query[...] = head_norm(total[:, :size], gain[0]).astype(query.dtype)
    pair[:, :size] = head_norm(total[:, size : 2 * size], gain[1]).astype(pair.dtype)
    pair[:, size:] = total[:, 2 * size :].astype(pair.dtype)


def headed(place, first, second, third, gains, theirs):
    rows, size = first.shape[0], gains.shape[1]
    return pl.pallas_call(
        head_kernel,
        out_shape=[
            jax.ShapeDtypeStruct((rows, size), jnp.bfloat16),
            jax.ShapeDtypeStruct((rows, 2 * size), jnp.bfloat16),
        ],
        in_specs=[SMALL] + [WHOLE] * 5,
        out_specs=[WHOLE] * 2,
        compiler_params=LIMIT,
        cost_estimate=pl.CostEstimate(flops=10 * first.size, bytes_accessed=4 * 2**19, transcendentals=0),
    )(place, first, second, third, gains, theirs)


def attention_kernel(tok_rows, place, sliced, query, near, far, out):
    rows, size = query.shape
    blks = sliced.shape[0]
    chips = rows // (blks * tok_rows)
    key = lax.broadcasted_iota(jnp.int32, (1, rows), 1)
    chip = sum((key >= i * blks * tok_rows).astype(jnp.int32) for i in range(1, chips))
    rest = key - chip * (blks * tok_rows)
    blk = sum((rest >= i * tok_rows).astype(jnp.int32) for i in range(1, blks))
    begin = chip * (2 * tok_rows) + rest - blk * tok_rows
    limit = jnp.zeros((1, rows), jnp.float32)
    for i in range(blks):
        count = sliced[i, tok_rows : tok_rows + 1, :1].astype(jnp.float32)
        limit = jnp.where(blk == i, count, limit)
    lanes = (place[1], 1 - place[1])
    valid = [(begin + lane * tok_rows).astype(jnp.float32) < limit for lane in lanes]
    pairs = (near, far)
    step = 2 * blks * tok_rows
    for part in range(rows // step):
        block = query[part * step : (part + 1) * step]
        scores = []
        for pair, mask in zip(pairs, valid):
            product = lax.dot_general(
                block, pair[:, :size], (((1,), (1,)), ((), ())), preferred_element_type=jnp.float32
            )
            scores.append(jnp.where(mask, product * (size**-0.5), -1e30))
        top = jnp.maximum(*(jnp.max(score, axis=-1, keepdims=True) for score in scores))
        denom, mixed = 0.0, 0.0
        for score, pair in zip(scores, pairs):
            expo = jnp.exp(score - top)
            denom += jnp.sum(expo, axis=-1, keepdims=True)
            mixed += jnp.dot(
                expo.astype(jnp.bfloat16), pair[:, size:], preferred_element_type=jnp.float32
            )
        mixed = mixed / denom
        for i in range(2):
            for j in range(blks):
                piece = mixed[(i * blks + j) * tok_rows : (i * blks + j + 1) * tok_rows]
                out[j * chips + 2 * part + i] = piece.astype(out.dtype)


def attended(tok_rows, place, sliced, query, near, far):
    rows, size = query.shape
    return pl.pallas_call(
        lambda *refs: attention_kernel(tok_rows, *refs),
        out_shape=jax.ShapeDtypeStruct((rows // tok_rows, tok_rows, size), jnp.bfloat16),
        in_specs=[SMALL] + [WHOLE] * 4,
        out_specs=WHOLE,
        compiler_params=LIMIT,
        cost_estimate=pl.CostEstimate(
            flops=8 * rows * rows * size, bytes_accessed=2**20, transcendentals=2 * rows * rows
        ),
    )(place, sliced, query, near, far)


def merge_kernel(blocks, out):
    blks, chips = blocks.shape[:2]
    size = blocks.shape[3]
    heads = out.shape[2] // (chips * size)
    for chip in range(chips):
        for blk in range(heads):
            begin = (chip * heads + blk) * size
            out[0, :, begin : begin + size] = blocks[blk, chip]


def merged(blocks, shape):
    return pl.pallas_call(
        merge_kernel,
        out_shape=jax.ShapeDtypeStruct(shape, blocks.dtype),
        in_specs=[WHOLE],
        out_specs=WHOLE,
        compiler_params=LIMIT,
        cost_estimate=pl.CostEstimate(flops=0, bytes_accessed=2**19, transcendentals=0),
    )(blocks)


def on_device(stale, layer_of_section, mod_table, w_qkv, q_gain, k_gain, counts):
    tok_rows, width = stale.shape[1:]
    blks = lax.axis_size("blk")
    chips = lax.axis_size("zlo") * lax.axis_size("x")
    slice_width, head_size = w_qkv.shape[1], w_qkv.shape[4]

    received = shifted(stale[0], "section", 1)
    modul = lax.dynamic_index_in_dim(mod_table, layer_of_section[0], 0, keepdims=False)
    place = jnp.stack([lax.axis_index("blk"), lax.axis_index("core")]).astype(jnp.int32)

    own = w_qkv[0].transpose(1, 2, 0, 3)
    gains = stacked(q_gain.transpose(1, 0, 2), k_gain.transpose(1, 0, 2))
    other = shifted(own, "core", 1)
    theirs = shifted(gains, "core", 1)

    sent = packed(counts, place, received, modul, (blks, 16, slice_width))
    sliced = lax.all_to_all(sent, "blk", 0, 0, tiled=False)
    copies = spread(sliced, other, (chips, blks * tok_rows, slice_width))
    tokens = lax.all_to_all(copies, CHIPS, 0, 0, tiled=False)
    tokens = tokens.reshape(chips * blks * tok_rows, slice_width)
    half = tokens.shape[0] // 2

    up, down = products((4,), place, tokens, own, other, 2)
    up, down = shifted(up, "blk", 1), shifted(down, "blk", -1)
    three, five = products((3, 5), place, tokens, own, other)
    up, down = shifted(added(three, up), "blk", 1), shifted(added(five, down, half), "blk", -1)
    two, six, one, seven, zero = products((2, 6, 1, 7, 0), place, tokens, own, other)
    up, down = shifted(added(two, up), "blk", 1), shifted(added(six, down), "blk", -1)
    up, down = shifted(added(one, up), "blk", 1), shifted(added(seven, down), "blk", -1)
    query, near = headed(place, zero, up, down, gains, theirs)
    far = shifted(near, "core", 1)

    mixed = attended(tok_rows, place, sliced, query, near, far)
    returned = lax.all_to_all(mixed, ("blk",) + CHIPS, 0, 0, tiled=False)
    return merged(returned.reshape(blks, chips, tok_rows, head_size), (1, tok_rows, width))


def solution(mesh):
    sizes = mesh.shape
    fine = Mesh(mesh.devices.reshape(sizes["section"], sizes["blk"], 2, 4, 2), AXES)
    uly = CHIPS + ("core",)
    in_specs = (
        P("section", ("blk",) + uly, None),
        P("section"),
        P(),
        P("section", "blk", uly, None, None),
        P("section", uly, None),
        P("section", uly, None),
        P("blk"),
    )
    out_specs = P("section", ("blk",) + uly, None)
    return jax.shard_map(
        on_device, mesh=fine, in_specs=in_specs, out_specs=out_specs, check_vma=False
    )
```

```python
import jax
import jax.numpy as jnp
from jax import lax
from jax.experimental import pallas as pl
from jax.experimental.pallas import tpu as pltpu
from jax.sharding import Mesh
from jax.sharding import PartitionSpec as P

AXES = ("section", "blk", "zlo", "x", "core")
CHIPS = ("zlo", "x")
SMALL = pl.BlockSpec(memory_space=pltpu.SMEM)
WHOLE = pl.BlockSpec(memory_space=pltpu.VMEM)
DISTANT = pl.BlockSpec(memory_space=pltpu.HBM)
LIMIT = pltpu.CompilerParams(vmem_limit_bytes=12 * 2**20)


def shifted(value, axis, steps):
    count = lax.axis_size(axis)
    pairs = [(source, (source + steps) % count) for source in range(count)]
    return lax.ppermute(value, axis, pairs)


def head_norm(values, gain):
    return values * lax.rsqrt(jnp.mean(values * values, axis=-1, keepdims=True) + 1e-06) * gain


def stack_kernel(q_gain, k_gain, gains):
    heads = q_gain.shape[0]
    for head in range(heads):
        gains[head : head + 1] = q_gain[head]
        gains[heads + head : heads + head + 1] = k_gain[head]


def stacked(q_gain, k_gain):
    return pl.pallas_call(
        stack_kernel,
        out_shape=jax.ShapeDtypeStruct((2 * q_gain.shape[0], q_gain.shape[2]), jnp.float32),
        in_specs=[WHOLE, WHOLE],
        out_specs=WHOLE,
        compiler_params=LIMIT,
        cost_estimate=pl.CostEstimate(flops=0, bytes_accessed=2**14, transcendentals=0),
    )(q_gain, k_gain)


def dense_kernel(stale, out, buffer):
    depth = out.shape[2] * 3 // 4
    piece = depth // 3
    for blk in range(out.shape[0]):
        block = stale[0, :, blk * depth : (blk + 1) * depth].astype(jnp.float32)
        buffer[blk, :, :depth] = block[:8]
        buffer[blk, 6:, depth:] = jnp.zeros((2, piece), jnp.float32)
        for token in range(2):
            for part in range(3):
                at = 3 * token + part
                buffer[blk, at : at + 1, depth:] = block[
                    8 + token : 9 + token, part * piece : (part + 1) * piece
                ]
    out[...] = buffer[...].astype(out.dtype)


def dense(stale, shape):
    return pl.pallas_call(
        dense_kernel,
        out_shape=jax.ShapeDtypeStruct(shape, jnp.bfloat16),
        in_specs=[WHOLE],
        out_specs=WHOLE,
        scratch_shapes=[pltpu.VMEM(shape, jnp.float32)],
        compiler_params=LIMIT,
        cost_estimate=pl.CostEstimate(flops=10**6, bytes_accessed=10**6, transcendentals=0),
    )(stale)


def norm_kernel(counts, place, stale, modul, out):
    blks, _, lanes = stale.shape
    depth = lanes * 3 // 4
    piece = depth // 3
    width = blks * depth
    source = stale[...].astype(jnp.float32)
    square = jnp.sum(source * source, axis=0)
    row = lax.broadcasted_iota(jnp.int32, (8, 1), 0)
    first = jnp.sum(square[:, :depth], axis=-1, keepdims=True)
    rest = jnp.sum(square[:, depth:], axis=-1, keepdims=True)
    eighth = jnp.sum(jnp.where(row < 3, rest, 0.0), axis=0, keepdims=True)
    ninth = jnp.sum(jnp.where((row >= 3) & (row < 6), rest, 0.0), axis=0, keepdims=True)
    spread = jnp.sqrt(first / width + 1e-06)
    last = jnp.sqrt(jnp.where(row < 3, eighth, ninth) / width + 1e-06)
    part = jnp.where(row < 3, row, row - 3)
    count = jnp.full((8, piece), counts[0], jnp.int32).astype(jnp.float32)
    for blk in range(blks):
        begin = blk * depth
        shift, scale = (modul[i : i + 1, begin : begin + depth] for i in (0, 1))
        normed = source[blk, :, :depth] / spread * (1.0 + scale) + shift
        out[blk, :, :depth] = normed.astype(out.dtype)
        shift, scale = (
            jnp.where(
                part == 0,
                values[:, :piece],
                jnp.where(part == 1, values[:, piece : 2 * piece], values[:, 2 * piece :]),
            )
            for values in (shift, scale)
        )
        normed = source[blk, :, depth:] / last * (1.0 + scale) + shift
        out[blk, :, depth:] = jnp.where(row < 6, normed, count).astype(out.dtype)


def normed(counts, place, stale, modul):
    return pl.pallas_call(
        norm_kernel,
        out_shape=jax.ShapeDtypeStruct(stale.shape, jnp.bfloat16),
        in_specs=[SMALL, SMALL, WHOLE, WHOLE],
        out_specs=WHOLE,
        compiler_params=LIMIT,
        cost_estimate=pl.CostEstimate(flops=10**10, bytes_accessed=10**6, transcendentals=0),
    )(counts, place, stale, modul)


def spread_kernel(sliced, weights, out, rows):
    blks, _, lanes = sliced.shape
    depth = lanes * 3 // 4
    piece = depth // 3
    tok_rows = rows.shape[0] // blks
    for blk in range(blks):
        block = sliced[blk].astype(jnp.float32)
        begin = blk * tok_rows
        rows[begin : begin + 8] = block[:, :depth]
        for token in range(2):
            for part in range(3):
                at = 3 * token + part
                rows[begin + 8 + token : begin + 9 + token, part * piece : (part + 1) * piece] = block[
                    at : at + 1, depth:
                ]
    block = rows[...].astype(out.dtype)
    for chip in range(out.shape[0]):
        out[chip] = block


def spread(sliced, weights, shape):
    return pl.pallas_call(
        spread_kernel,
        out_shape=jax.ShapeDtypeStruct(shape, jnp.bfloat16),
        in_specs=[WHOLE, DISTANT],
        out_specs=WHOLE,
        scratch_shapes=[pltpu.VMEM(shape[1:], jnp.float32)],
        compiler_params=LIMIT,
        cost_estimate=pl.CostEstimate(flops=0, bytes_accessed=10**6, transcendentals=0),
    )(sliced, weights)


def product_kernel(steps, place, tokens, own, other, *refs):
    outs, block, sems = refs[:-2], refs[-2], refs[-1]
    pieces = len(outs) // len(steps)
    size = tokens.shape[0] // pieces
    row, core = place[0], place[1]
    heads, parts = own.shape[:2]

    def fetch(number):
        owner = lax.rem(row + steps[number], lax.axis_size("blk"))
        head = jnp.minimum(owner, 2 * heads - 1)
        lane = jnp.where(head >= heads, 1, 0)
        slot = number % 2

        @pl.when(lane == core)
        def _():
            pltpu.make_async_copy(own.at[head - lane * heads], block.at[slot], sems.at[slot]).start()

        @pl.when(lane != core)
        def _():
            pltpu.make_async_copy(other.at[head - lane * heads], block.at[slot], sems.at[slot]).start()

    fetch(0)
    for number in range(len(steps)):
        slot = number % 2
        if number + 1 < len(steps):
            fetch(number + 1)
        pltpu.make_async_copy(own.at[0], block.at[slot], sems.at[slot]).wait()
        weights = jnp.concatenate([block[slot, part] for part in range(parts)], axis=1)
        total = jnp.dot(tokens[...], weights, preferred_element_type=jnp.float32)
        for piece in range(pieces):
            out = outs[number * pieces + piece]
            out[...] = total[piece * size : (piece + 1) * size].astype(out.dtype)


def products(steps, place, tokens, own, other, pieces=1):
    rows, depth = tokens.shape
    parts, size = own.shape[1], own.shape[3]
    shape = jax.ShapeDtypeStruct((rows // pieces, parts * size), jnp.bfloat16)
    return pl.pallas_call(
        lambda *refs: product_kernel(steps, *refs),
        out_shape=[shape] * (pieces * len(steps)),
        in_specs=[SMALL, WHOLE, DISTANT, DISTANT],
        out_specs=[WHOLE] * (pieces * len(steps)),
        scratch_shapes=[
            pltpu.VMEM((2,) + own.shape[1:], jnp.bfloat16),
            pltpu.SemaphoreType.DMA((2,)),
        ],
        compiler_params=LIMIT,
        cost_estimate=pl.CostEstimate(
            flops=2 * rows * depth * parts * size * len(steps), bytes_accessed=4 * 2**20, transcendentals=0
        ),
    )(place, tokens, own, other)


def add_kernel(begin, first, second, out):
    rows = second.shape[0]
    total = first[begin : begin + rows].astype(jnp.float32) + second[...].astype(jnp.float32)
    out[begin : begin + rows] = total.astype(out.dtype)
    for low, high in ((0, begin), (begin + rows, out.shape[0])):
        if high > low:
            out[low:high] = first[low:high]


def added(first, second, begin=0):
    return pl.pallas_call(
        lambda *refs: add_kernel(begin, *refs),
        out_shape=jax.ShapeDtypeStruct(first.shape, first.dtype),
        in_specs=[WHOLE, WHOLE],
        out_specs=WHOLE,
        compiler_params=LIMIT,
        cost_estimate=pl.CostEstimate(flops=first.size, bytes_accessed=3 * 2**19, transcendentals=0),
    )(first, second)


def head_kernel(place, first, second, third, gains, theirs, query, pair):
    size = query.shape[1]
    heads = gains.shape[0] // 2
    owned = jnp.minimum(place[0], 2 * heads - 1)
    lane = jnp.where(owned >= heads, 1, 0)
    index = owned - lane * heads
    mine = lane == place[1]
    gain = []
    for part in range(2):
        at = pl.ds(part * heads + index, 1)
        gain.append(jnp.where(mine, gains[at], theirs[at]))
    total = first[...].astype(jnp.float32) + second[...].astype(jnp.float32)
    total = total + third[...].astype(jnp.float32)
    query[...] = head_norm(total[:, :size], gain[0]).astype(query.dtype)
    pair[:, :size] = head_norm(total[:, size : 2 * size], gain[1]).astype(pair.dtype)
    pair[:, size:] = total[:, 2 * size :].astype(pair.dtype)


def headed(place, first, second, third, gains, theirs):
    rows, size = first.shape[0], gains.shape[1]
    return pl.pallas_call(
        head_kernel,
        out_shape=[
            jax.ShapeDtypeStruct((rows, size), jnp.bfloat16),
            jax.ShapeDtypeStruct((rows, 2 * size), jnp.bfloat16),
        ],
        in_specs=[SMALL] + [WHOLE] * 5,
        out_specs=[WHOLE] * 2,
        compiler_params=LIMIT,
        cost_estimate=pl.CostEstimate(flops=10 * first.size, bytes_accessed=4 * 2**19, transcendentals=0),
    )(place, first, second, third, gains, theirs)


def attention_kernel(tok_rows, place, sliced, query, near, far, out, mixed):
    rows, size = query.shape
    blks = sliced.shape[0]
    chips = rows // (blks * tok_rows)
    key = lax.broadcasted_iota(jnp.int32, (1, rows), 1)
    chip = sum((key >= i * blks * tok_rows).astype(jnp.int32) for i in range(1, chips))
    rest = key - chip * (blks * tok_rows)
    blk = sum((rest >= i * tok_rows).astype(jnp.int32) for i in range(1, blks))
    begin = chip * (2 * tok_rows) + rest - blk * tok_rows
    limit = jnp.zeros((1, rows), jnp.float32)
    for i in range(blks):
        count = sliced[i, -2:, -1:][:1].astype(jnp.float32)
        limit = jnp.where(blk == i, count, limit)
    lanes = (place[1], 1 - place[1])
    valid = [(begin + lane * tok_rows).astype(jnp.float32) < limit for lane in lanes]
    pairs = (near, far)
    scores = []
    for pair, mask in zip(pairs, valid):
        product = lax.dot_general(
            query[...], pair[:, :size], (((1,), (1,)), ((), ())), preferred_element_type=jnp.float32
        )
        scores.append(jnp.where(mask, product * (size**-0.5), -1e30))
    top = jnp.maximum(*(jnp.max(score, axis=-1, keepdims=True) for score in scores))
    denom, total = 0.0, 0.0
    for score, pair in zip(scores, pairs):
        expo = jnp.exp(score - top)
        denom += jnp.sum(expo, axis=-1, keepdims=True)
        total += jnp.dot(expo.astype(jnp.bfloat16), pair[:, size:], preferred_element_type=jnp.float32)
    mixed[...] = total / denom
    for i in range(chips):
        for j in range(blks):
            begin = (i * blks + j) * tok_rows
            out[j * chips + i] = mixed[begin : begin + tok_rows].astype(out.dtype)


def attended(tok_rows, place, sliced, query, near, far):
    rows, size = query.shape
    return pl.pallas_call(
        lambda *refs: attention_kernel(tok_rows, *refs),
        out_shape=jax.ShapeDtypeStruct((rows // tok_rows, tok_rows, size), jnp.bfloat16),
        in_specs=[SMALL] + [WHOLE] * 4,
        out_specs=WHOLE,
        scratch_shapes=[pltpu.VMEM((rows, size), jnp.float32)],
        compiler_params=LIMIT,
        cost_estimate=pl.CostEstimate(
            flops=8 * rows * rows * size, bytes_accessed=2**20, transcendentals=2 * rows * rows
        ),
    )(place, sliced, query, near, far)


def merge_kernel(blocks, out):
    blks, chips = blocks.shape[:2]
    size = blocks.shape[3]
    heads = out.shape[2] // (chips * size)
    for chip in range(chips):
        for blk in range(heads):
            begin = (chip * heads + blk) * size
            out[0, :, begin : begin + size] = blocks[blk, chip]


def merged(blocks, shape):
    return pl.pallas_call(
        merge_kernel,
        out_shape=jax.ShapeDtypeStruct(shape, blocks.dtype),
        in_specs=[WHOLE],
        out_specs=WHOLE,
        compiler_params=LIMIT,
        cost_estimate=pl.CostEstimate(flops=0, bytes_accessed=2**19, transcendentals=0),
    )(blocks)


def on_device(stale, layer_of_section, mod_table, w_qkv, q_gain, k_gain, counts):
    tok_rows, width = stale.shape[1:]
    blks = lax.axis_size("blk")
    chips = lax.axis_size("zlo") * lax.axis_size("x")
    slice_width, head_size = w_qkv.shape[1], w_qkv.shape[4]

    received = shifted(dense(stale, (blks, 8, slice_width * 4 // 3)), "section", 1)
    modul = lax.dynamic_index_in_dim(mod_table, layer_of_section[0], 0, keepdims=False)
    place = jnp.stack([lax.axis_index("blk"), lax.axis_index("core")]).astype(jnp.int32)

    own = w_qkv[0].transpose(1, 2, 0, 3)
    gains = stacked(q_gain.transpose(1, 0, 2), k_gain.transpose(1, 0, 2))
    other = shifted(own, "core", 1)
    theirs = shifted(gains, "core", 1)

    sent = normed(counts, place, received, modul)
    sliced = lax.all_to_all(sent, "blk", 0, 0, tiled=False)
    copies = spread(sliced, other, (chips, blks * tok_rows, slice_width))
    tokens = lax.all_to_all(copies, CHIPS, 0, 0, tiled=False)
    tokens = tokens.reshape(chips * blks * tok_rows, slice_width)
    half = tokens.shape[0] // 2

    up, down = products((4,), place, tokens, own, other, 2)
    up, down = shifted(up, "blk", 1), shifted(down, "blk", -1)
    three, five = products((3, 5), place, tokens, own, other)
    up, down = shifted(added(three, up), "blk", 1), shifted(added(five, down, half), "blk", -1)
    two, six, one, seven, zero = products((2, 6, 1, 7, 0), place, tokens, own, other)
    up, down = shifted(added(two, up), "blk", 1), shifted(added(six, down), "blk", -1)
    up, down = shifted(added(one, up), "blk", 1), shifted(added(seven, down), "blk", -1)
    query, near = headed(place, zero, up, down, gains, theirs)
    far = shifted(near, "core", 1)

    mixed = attended(tok_rows, place, sliced, query, near, far)
    returned = lax.all_to_all(mixed, ("blk",) + CHIPS, 0, 0, tiled=False)
    return merged(returned.reshape(blks, chips, tok_rows, head_size), (1, tok_rows, width))


def solution(mesh):
    sizes = mesh.shape
    fine = Mesh(mesh.devices.reshape(sizes["section"], sizes["blk"], 2, 4, 2), AXES)
    uly = CHIPS + ("core",)
    in_specs = (
        P("section", ("blk",) + uly, None),
        P("section"),
        P(),
        P("section", "blk", uly, None, None),
        P("section", uly, None),
        P("section", uly, None),
        P("blk"),
    )
    out_specs = P("section", ("blk",) + uly, None)
    return jax.shard_map(
        on_device, mesh=fine, in_specs=in_specs, out_specs=out_specs, check_vma=False
    )
```

```python
import jax
import jax.numpy as jnp
from jax import lax
from jax.experimental import pallas as pl
from jax.experimental.pallas import tpu as pltpu
from jax.sharding import Mesh
from jax.sharding import PartitionSpec as P

AXES = ("section", "blk", "zlo", "x", "core")
CHIPS = ("zlo", "x")
SMALL = pl.BlockSpec(memory_space=pltpu.SMEM)
WHOLE = pl.BlockSpec(memory_space=pltpu.VMEM)
DISTANT = pl.BlockSpec(memory_space=pltpu.HBM)
LIMIT = pltpu.CompilerParams(vmem_limit_bytes=12 * 2**20)


def shifted(value, axis, steps):
    count = lax.axis_size(axis)
    pairs = [(source, (source + steps) % count) for source in range(count)]
    return lax.ppermute(value, axis, pairs)


def passed(value, steps, ahead, owners):
    blks = lax.axis_size("blk")
    pairs = [(row, (row + steps) % blks) for row in range(blks) if (row + steps * ahead) % blks < owners]
    return lax.ppermute(value, "blk", pairs)


def head_norm(values, gain):
    return values * lax.rsqrt(jnp.mean(values * values, axis=-1, keepdims=True) + 1e-06) * gain


def stack_kernel(q_gain, k_gain, gains):
    heads = q_gain.shape[0]
    for head in range(heads):
        gains[head : head + 1] = q_gain[head]
        gains[heads + head : heads + head + 1] = k_gain[head]


def stacked(q_gain, k_gain):
    return pl.pallas_call(
        stack_kernel,
        out_shape=jax.ShapeDtypeStruct((2 * q_gain.shape[0], q_gain.shape[2]), jnp.float32),
        in_specs=[WHOLE, WHOLE],
        out_specs=WHOLE,
        compiler_params=LIMIT,
        cost_estimate=pl.CostEstimate(flops=0, bytes_accessed=2**14, transcendentals=0),
    )(q_gain, k_gain)


def dense_kernel(stale, out, buffer):
    depth = out.shape[2] * 3 // 4
    piece = depth // 3
    for blk in range(out.shape[0]):
        block = stale[0, :, blk * depth : (blk + 1) * depth].astype(jnp.float32)
        buffer[blk, :, :depth] = block[:8]
        buffer[blk, 6:, depth:] = jnp.zeros((2, piece), jnp.float32)
        for token in range(2):
            for part in range(3):
                at = 3 * token + part
                buffer[blk, at : at + 1, depth:] = block[
                    8 + token : 9 + token, part * piece : (part + 1) * piece
                ]
    out[...] = buffer[...].astype(out.dtype)


def dense(stale, shape):
    return pl.pallas_call(
        dense_kernel,
        out_shape=jax.ShapeDtypeStruct(shape, jnp.bfloat16),
        in_specs=[WHOLE],
        out_specs=WHOLE,
        scratch_shapes=[pltpu.VMEM(shape, jnp.float32)],
        compiler_params=LIMIT,
        cost_estimate=pl.CostEstimate(flops=10**6, bytes_accessed=10**6, transcendentals=0),
    )(stale)


def norm_kernel(counts, place, stale, modul, out):
    blks, _, lanes = stale.shape
    depth = lanes * 3 // 4
    piece = depth // 3
    width = blks * depth
    source = stale[...].astype(jnp.float32)
    square = jnp.sum(source * source, axis=0)
    row = lax.broadcasted_iota(jnp.int32, (8, 1), 0)
    first = jnp.sum(square[:, :depth], axis=-1, keepdims=True)
    rest = jnp.sum(square[:, depth:], axis=-1, keepdims=True)
    eighth = jnp.sum(jnp.where(row < 3, rest, 0.0), axis=0, keepdims=True)
    ninth = jnp.sum(jnp.where((row >= 3) & (row < 6), rest, 0.0), axis=0, keepdims=True)
    spread = jnp.sqrt(first / width + 1e-06)
    last = jnp.sqrt(jnp.where(row < 3, eighth, ninth) / width + 1e-06)
    part = jnp.where(row < 3, row, row - 3)
    count = jnp.full((8, piece), counts[0], jnp.int32).astype(jnp.float32)
    for blk in range(blks):
        begin = blk * depth
        shift, scale = (modul[i : i + 1, begin : begin + depth] for i in (0, 1))
        normed = source[blk, :, :depth] / spread * (1.0 + scale) + shift
        out[blk, :, :depth] = normed.astype(out.dtype)
        shift, scale = (
            jnp.where(
                part == 0,
                values[:, :piece],
                jnp.where(part == 1, values[:, piece : 2 * piece], values[:, 2 * piece :]),
            )
            for values in (shift, scale)
        )
        normed = source[blk, :, depth:] / last * (1.0 + scale) + shift
        out[blk, :, depth:] = jnp.where(row < 6, normed, count).astype(out.dtype)


def normed(counts, place, stale, modul):
    return pl.pallas_call(
        norm_kernel,
        out_shape=jax.ShapeDtypeStruct(stale.shape, jnp.bfloat16),
        in_specs=[SMALL, SMALL, WHOLE, WHOLE],
        out_specs=WHOLE,
        compiler_params=LIMIT,
        cost_estimate=pl.CostEstimate(flops=10**10, bytes_accessed=10**6, transcendentals=0),
    )(counts, place, stale, modul)


def spread_kernel(sliced, weights, out, rows):
    blks, _, lanes = sliced.shape
    depth = lanes * 3 // 4
    piece = depth // 3
    tok_rows = rows.shape[0] // blks
    for blk in range(blks):
        block = sliced[blk].astype(jnp.float32)
        begin = blk * tok_rows
        rows[begin : begin + 8] = block[:, :depth]
        for token in range(2):
            for part in range(3):
                at = 3 * token + part
                rows[begin + 8 + token : begin + 9 + token, part * piece : (part + 1) * piece] = block[
                    at : at + 1, depth:
                ]
    block = rows[...].astype(out.dtype)
    for chip in range(out.shape[0]):
        out[chip] = block


def spread(sliced, weights, shape):
    return pl.pallas_call(
        spread_kernel,
        out_shape=jax.ShapeDtypeStruct(shape, jnp.bfloat16),
        in_specs=[WHOLE, DISTANT],
        out_specs=WHOLE,
        scratch_shapes=[pltpu.VMEM(shape[1:], jnp.float32)],
        compiler_params=LIMIT,
        cost_estimate=pl.CostEstimate(flops=0, bytes_accessed=10**6, transcendentals=0),
    )(sliced, weights)


def product_kernel(steps, place, tokens, own, other, *refs):
    outs, block, sems = refs[:-2], refs[-2], refs[-1]
    pieces = len(outs) // len(steps)
    size = tokens.shape[0] // pieces
    row, core = place[0], place[1]
    heads, parts = own.shape[:2]

    def fetch(number):
        owner = lax.rem(row + steps[number], lax.axis_size("blk"))
        head = jnp.minimum(owner, 2 * heads - 1)
        lane = jnp.where(head >= heads, 1, 0)
        slot = number % 2

        @pl.when(lane == core)
        def _():
            pltpu.make_async_copy(own.at[head - lane * heads], block.at[slot], sems.at[slot]).start()

        @pl.when(lane != core)
        def _():
            pltpu.make_async_copy(other.at[head - lane * heads], block.at[slot], sems.at[slot]).start()

    fetch(0)
    for number in range(len(steps)):
        slot = number % 2
        if number + 1 < len(steps):
            fetch(number + 1)
        pltpu.make_async_copy(own.at[0], block.at[slot], sems.at[slot]).wait()
        weights = jnp.concatenate([block[slot, part] for part in range(parts)], axis=1)
        total = jnp.dot(tokens[...], weights, preferred_element_type=jnp.float32)
        for piece in range(pieces):
            out = outs[number * pieces + piece]
            out[...] = total[piece * size : (piece + 1) * size].astype(out.dtype)


def products(steps, place, tokens, own, other, pieces=1):
    rows, depth = tokens.shape
    parts, size = own.shape[1], own.shape[3]
    shape = jax.ShapeDtypeStruct((rows // pieces, parts * size), jnp.bfloat16)
    return pl.pallas_call(
        lambda *refs: product_kernel(steps, *refs),
        out_shape=[shape] * (pieces * len(steps)),
        in_specs=[SMALL, WHOLE, DISTANT, DISTANT],
        out_specs=[WHOLE] * (pieces * len(steps)),
        scratch_shapes=[
            pltpu.VMEM((2,) + own.shape[1:], jnp.bfloat16),
            pltpu.SemaphoreType.DMA((2,)),
        ],
        compiler_params=LIMIT,
        cost_estimate=pl.CostEstimate(
            flops=2 * rows * depth * parts * size * len(steps), bytes_accessed=4 * 2**20, transcendentals=0
        ),
    )(place, tokens, own, other)


def add_kernel(begin, first, second, out):
    rows = second.shape[0]
    total = first[begin : begin + rows].astype(jnp.float32) + second[...].astype(jnp.float32)
    out[begin : begin + rows] = total.astype(out.dtype)
    for low, high in ((0, begin), (begin + rows, out.shape[0])):
        if high > low:
            out[low:high] = first[low:high]


def added(first, second, begin=0):
    return pl.pallas_call(
        lambda *refs: add_kernel(begin, *refs),
        out_shape=jax.ShapeDtypeStruct(first.shape, first.dtype),
        in_specs=[WHOLE, WHOLE],
        out_specs=WHOLE,
        compiler_params=LIMIT,
        cost_estimate=pl.CostEstimate(flops=first.size, bytes_accessed=3 * 2**19, transcendentals=0),
    )(first, second)


def head_kernel(place, first, second, third, gains, theirs, query, pair):
    size = query.shape[1]
    heads = gains.shape[0] // 2
    owned = jnp.minimum(place[0], 2 * heads - 1)
    lane = jnp.where(owned >= heads, 1, 0)
    index = owned - lane * heads
    mine = lane == place[1]
    gain = []
    for part in range(2):
        at = pl.ds(part * heads + index, 1)
        gain.append(jnp.where(mine, gains[at], theirs[at]))
    total = first[...].astype(jnp.float32) + second[...].astype(jnp.float32)
    total = total + third[...].astype(jnp.float32)
    query[...] = head_norm(total[:, :size], gain[0]).astype(query.dtype)
    pair[:, :size] = head_norm(total[:, size : 2 * size], gain[1]).astype(pair.dtype)
    pair[:, size:] = total[:, 2 * size :].astype(pair.dtype)


def headed(place, first, second, third, gains, theirs):
    rows, size = first.shape[0], gains.shape[1]
    return pl.pallas_call(
        head_kernel,
        out_shape=[
            jax.ShapeDtypeStruct((rows, size), jnp.bfloat16),
            jax.ShapeDtypeStruct((rows, 2 * size), jnp.bfloat16),
        ],
        in_specs=[SMALL] + [WHOLE] * 5,
        out_specs=[WHOLE] * 2,
        compiler_params=LIMIT,
        cost_estimate=pl.CostEstimate(flops=10 * first.size, bytes_accessed=4 * 2**19, transcendentals=0),
    )(place, first, second, third, gains, theirs)


def attention_kernel(tok_rows, place, sliced, query, near, far, out, mixed):
    rows, size = query.shape
    blks = sliced.shape[0]
    chips = rows // (blks * tok_rows)
    key = lax.broadcasted_iota(jnp.int32, (1, rows), 1)
    chip = sum((key >= i * blks * tok_rows).astype(jnp.int32) for i in range(1, chips))
    rest = key - chip * (blks * tok_rows)
    blk = sum((rest >= i * tok_rows).astype(jnp.int32) for i in range(1, blks))
    begin = chip * (2 * tok_rows) + rest - blk * tok_rows
    limit = jnp.zeros((1, rows), jnp.float32)
    for i in range(blks):
        count = sliced[i, -2:, -1:][:1].astype(jnp.float32)
        limit = jnp.where(blk == i, count, limit)
    lanes = (place[1], 1 - place[1])
    valid = [(begin + lane * tok_rows).astype(jnp.float32) < limit for lane in lanes]
    pairs = (near, far)
    scores = []
    for pair, mask in zip(pairs, valid):
        product = lax.dot_general(
            query[...], pair[:, :size], (((1,), (1,)), ((), ())), preferred_element_type=jnp.float32
        )
        scores.append(jnp.where(mask, product * (size**-0.5), -1e30))
    top = jnp.maximum(*(jnp.max(score, axis=-1, keepdims=True) for score in scores))
    denom, total = 0.0, 0.0
    for score, pair in zip(scores, pairs):
        expo = jnp.exp(score - top)
        denom += jnp.sum(expo, axis=-1, keepdims=True)
        total += jnp.dot(expo.astype(jnp.bfloat16), pair[:, size:], preferred_element_type=jnp.float32)
    mixed[...] = total / denom
    for i in range(chips):
        for j in range(blks):
            begin = (i * blks + j) * tok_rows
            out[j * chips + i] = mixed[begin : begin + tok_rows].astype(out.dtype)


def attended(tok_rows, place, sliced, query, near, far):
    rows, size = query.shape
    return pl.pallas_call(
        lambda *refs: attention_kernel(tok_rows, *refs),
        out_shape=jax.ShapeDtypeStruct((rows // tok_rows, tok_rows, size), jnp.bfloat16),
        in_specs=[SMALL] + [WHOLE] * 4,
        out_specs=WHOLE,
        scratch_shapes=[pltpu.VMEM((rows, size), jnp.float32)],
        compiler_params=LIMIT,
        cost_estimate=pl.CostEstimate(
            flops=8 * rows * rows * size, bytes_accessed=2**20, transcendentals=2 * rows * rows
        ),
    )(place, sliced, query, near, far)


def merge_kernel(blocks, out):
    blks, chips = blocks.shape[:2]
    size = blocks.shape[3]
    heads = out.shape[2] // (chips * size)
    for chip in range(chips):
        for blk in range(heads):
            begin = (chip * heads + blk) * size
            out[0, :, begin : begin + size] = blocks[blk, chip]


def merged(blocks, shape):
    return pl.pallas_call(
        merge_kernel,
        out_shape=jax.ShapeDtypeStruct(shape, blocks.dtype),
        in_specs=[WHOLE],
        out_specs=WHOLE,
        compiler_params=LIMIT,
        cost_estimate=pl.CostEstimate(flops=0, bytes_accessed=2**19, transcendentals=0),
    )(blocks)


def on_device(stale, layer_of_section, mod_table, w_qkv, q_gain, k_gain, counts):
    tok_rows, width = stale.shape[1:]
    blks = lax.axis_size("blk")
    chips = lax.axis_size("zlo") * lax.axis_size("x")
    slice_width, head_size = w_qkv.shape[1], w_qkv.shape[4]

    received = shifted(dense(stale, (blks, 8, slice_width * 4 // 3)), "section", 1)
    modul = lax.dynamic_index_in_dim(mod_table, layer_of_section[0], 0, keepdims=False)
    place = jnp.stack([lax.axis_index("blk"), lax.axis_index("core")]).astype(jnp.int32)

    own = w_qkv[0].transpose(1, 2, 0, 3)
    gains = stacked(q_gain.transpose(1, 0, 2), k_gain.transpose(1, 0, 2))
    other = shifted(own, "core", 1)
    theirs = shifted(gains, "core", 1)

    sent = normed(counts, place, received, modul)
    sliced = lax.all_to_all(sent, "blk", 0, 0, tiled=False)
    copies = spread(sliced, other, (chips, blks * tok_rows, slice_width))
    tokens = lax.all_to_all(copies, CHIPS, 0, 0, tiled=False)
    tokens = tokens.reshape(chips * blks * tok_rows, slice_width)
    half = tokens.shape[0] // 2

    owners = 2 * own.shape[0]
    up, down = products((4,), place, tokens, own, other, 2)
    up, down = passed(up, 1, 4, owners), passed(down, -1, 4, owners)
    three, five = products((3, 5), place, tokens, own, other)
    up, down = passed(added(three, up), 1, 3, owners), passed(added(five, down, half), -1, 3, owners)
    two, six, one, seven, zero = products((2, 6, 1, 7, 0), place, tokens, own, other)
    up, down = passed(added(two, up), 1, 2, owners), passed(added(six, down), -1, 2, owners)
    up, down = passed(added(one, up), 1, 1, owners), passed(added(seven, down), -1, 1, owners)
    query, near = headed(place, zero, up, down, gains, theirs)
    far = shifted(near, "core", 1)

    mixed = attended(tok_rows, place, sliced, query, near, far)
    returned = lax.all_to_all(mixed, ("blk",) + CHIPS, 0, 0, tiled=False)
    return merged(returned.reshape(blks, chips, tok_rows, head_size), (1, tok_rows, width))


def solution(mesh):
    sizes = mesh.shape
    fine = Mesh(mesh.devices.reshape(sizes["section"], sizes["blk"], 2, 4, 2), AXES)
    uly = CHIPS + ("core",)
    in_specs = (
        P("section", ("blk",) + uly, None),
        P("section"),
        P(),
        P("section", "blk", uly, None, None),
        P("section", uly, None),
        P("section", uly, None),
        P("blk"),
    )
    out_specs = P("section", ("blk",) + uly, None)
    return jax.shard_map(
        on_device, mesh=fine, in_specs=in_specs, out_specs=out_specs, check_vma=False
    )
```

```python
import jax
import jax.numpy as jnp
from jax import lax
from jax.experimental import pallas as pl
from jax.experimental.pallas import tpu as pltpu
from jax.sharding import Mesh
from jax.sharding import PartitionSpec as P

AXES = ("section", "blk", "zlo", "x", "core")
CHIPS = ("zlo", "x")
SMALL = pl.BlockSpec(memory_space=pltpu.SMEM)
WHOLE = pl.BlockSpec(memory_space=pltpu.VMEM)
DISTANT = pl.BlockSpec(memory_space=pltpu.HBM)
LIMIT = pltpu.CompilerParams(vmem_limit_bytes=12 * 2**20)


def shifted(value, axis, steps):
    count = lax.axis_size(axis)
    pairs = [(source, (source + steps) % count) for source in range(count)]
    return lax.ppermute(value, axis, pairs)


def passed(value, steps, ahead, owners):
    blks = lax.axis_size("blk")
    pairs = [(row, (row + steps) % blks) for row in range(blks) if (row + steps * ahead) % blks < owners]
    return lax.ppermute(value, "blk", pairs)


def head_norm(values, gain):
    return values * lax.rsqrt(jnp.mean(values * values, axis=-1, keepdims=True) + 1e-06) * gain


def stack_kernel(q_gain, k_gain, gains):
    heads = q_gain.shape[0]
    for head in range(heads):
        gains[head : head + 1] = q_gain[head]
        gains[heads + head : heads + head + 1] = k_gain[head]


def stacked(q_gain, k_gain):
    return pl.pallas_call(
        stack_kernel,
        out_shape=jax.ShapeDtypeStruct((2 * q_gain.shape[0], q_gain.shape[2]), jnp.float32),
        in_specs=[WHOLE, WHOLE],
        out_specs=WHOLE,
        compiler_params=LIMIT,
        cost_estimate=pl.CostEstimate(flops=0, bytes_accessed=2**14, transcendentals=0),
    )(q_gain, k_gain)


def dense_kernel(stale, out, buffer):
    depth = out.shape[2] * 3 // 4
    piece = depth // 3
    for blk in range(out.shape[0]):
        block = stale[0, :, blk * depth : (blk + 1) * depth].astype(jnp.float32)
        buffer[blk, :, :depth] = block[:8]
        buffer[blk, 6:, depth:] = jnp.zeros((2, piece), jnp.float32)
        for token in range(2):
            for part in range(3):
                at = 3 * token + part
                buffer[blk, at : at + 1, depth:] = block[
                    8 + token : 9 + token, part * piece : (part + 1) * piece
                ]
    out[...] = buffer[...].astype(out.dtype)


def dense(stale, shape):
    return pl.pallas_call(
        dense_kernel,
        out_shape=jax.ShapeDtypeStruct(shape, jnp.bfloat16),
        in_specs=[WHOLE],
        out_specs=WHOLE,
        scratch_shapes=[pltpu.VMEM(shape, jnp.float32)],
        compiler_params=LIMIT,
        cost_estimate=pl.CostEstimate(flops=10**6, bytes_accessed=10**6, transcendentals=0),
    )(stale)


def norm_kernel(counts, place, stale, modul, out):
    blks, _, lanes = stale.shape
    depth = lanes * 3 // 4
    piece = depth // 3
    width = blks * depth
    source = stale[...].astype(jnp.float32)
    square = jnp.sum(source * source, axis=0)
    row = lax.broadcasted_iota(jnp.int32, (8, 1), 0)
    first = jnp.sum(square[:, :depth], axis=-1, keepdims=True)
    rest = jnp.sum(square[:, depth:], axis=-1, keepdims=True)
    eighth = jnp.sum(jnp.where(row < 3, rest, 0.0), axis=0, keepdims=True)
    ninth = jnp.sum(jnp.where((row >= 3) & (row < 6), rest, 0.0), axis=0, keepdims=True)
    spread = jnp.sqrt(first / width + 1e-06)
    last = jnp.sqrt(jnp.where(row < 3, eighth, ninth) / width + 1e-06)
    part = jnp.where(row < 3, row, row - 3)
    count = jnp.full((8, piece), counts[0], jnp.int32).astype(jnp.float32)
    for blk in range(blks):
        begin = blk * depth
        shift, scale = (modul[i : i + 1, begin : begin + depth] for i in (0, 1))
        normed = source[blk, :, :depth] / spread * (1.0 + scale) + shift
        out[blk, :, :depth] = normed.astype(out.dtype)
        shift, scale = (
            jnp.where(
                part == 0,
                values[:, :piece],
                jnp.where(part == 1, values[:, piece : 2 * piece], values[:, 2 * piece :]),
            )
            for values in (shift, scale)
        )
        normed = source[blk, :, depth:] / last * (1.0 + scale) + shift
        out[blk, :, depth:] = jnp.where(row < 6, normed, count).astype(out.dtype)


def normed(counts, place, stale, modul):
    return pl.pallas_call(
        norm_kernel,
        out_shape=jax.ShapeDtypeStruct(stale.shape, jnp.bfloat16),
        in_specs=[SMALL, SMALL, WHOLE, WHOLE],
        out_specs=WHOLE,
        compiler_params=LIMIT,
        cost_estimate=pl.CostEstimate(flops=10**10, bytes_accessed=10**6, transcendentals=0),
    )(counts, place, stale, modul)


def spread_kernel(sliced, weights, out, rows):
    blks, _, lanes = sliced.shape
    depth = lanes * 3 // 4
    piece = depth // 3
    tok_rows = rows.shape[0] // blks
    for blk in range(blks):
        block = sliced[blk].astype(jnp.float32)
        begin = blk * tok_rows
        rows[begin : begin + 8] = block[:, :depth]
        for token in range(2):
            for part in range(3):
                at = 3 * token + part
                rows[begin + 8 + token : begin + 9 + token, part * piece : (part + 1) * piece] = block[
                    at : at + 1, depth:
                ]
    block = rows[...].astype(out.dtype)
    for chip in range(out.shape[0]):
        out[chip] = block


def spread(sliced, weights, shape):
    return pl.pallas_call(
        spread_kernel,
        out_shape=jax.ShapeDtypeStruct(shape, jnp.bfloat16),
        in_specs=[WHOLE, DISTANT],
        out_specs=WHOLE,
        scratch_shapes=[pltpu.VMEM(shape[1:], jnp.float32)],
        compiler_params=LIMIT,
        cost_estimate=pl.CostEstimate(flops=0, bytes_accessed=10**6, transcendentals=0),
    )(sliced, weights)


def product_kernel(steps, place, tokens, own, other, *refs):
    outs, block, sems = refs[:-2], refs[-2], refs[-1]
    pieces = len(outs) // len(steps)
    row, core = place[0], place[1]
    heads, parts = own.shape[:2]

    def fetch(number):
        owner = lax.rem(row + steps[number], lax.axis_size("blk"))
        head = jnp.minimum(owner, 2 * heads - 1)
        lane = jnp.where(head >= heads, 1, 0)
        slot = number % 2

        @pl.when(lane == core)
        def _():
            pltpu.make_async_copy(own.at[head - lane * heads], block.at[slot], sems.at[slot]).start()

        @pl.when(lane != core)
        def _():
            pltpu.make_async_copy(other.at[head - lane * heads], block.at[slot], sems.at[slot]).start()

    fetch(0)
    for number in range(len(steps)):
        slot = number % 2
        if number + 1 < len(steps):
            fetch(number + 1)
        pltpu.make_async_copy(own.at[0], block.at[slot], sems.at[slot]).wait()
        weights = jnp.concatenate([block[slot, part] for part in range(parts)], axis=1)
        total = jnp.dot(tokens[...], weights, preferred_element_type=jnp.float32)
        begin = 0
        for out in outs[number * pieces : (number + 1) * pieces]:
            out[...] = total[begin : begin + out.shape[0]].astype(out.dtype)
            begin += out.shape[0]


def products(steps, place, tokens, own, other, pieces=None):
    rows, depth = tokens.shape
    parts, size = own.shape[1], own.shape[3]
    pieces = pieces or (rows,)
    shapes = [jax.ShapeDtypeStruct((piece, parts * size), jnp.bfloat16) for piece in pieces]
    return pl.pallas_call(
        lambda *refs: product_kernel(steps, *refs),
        out_shape=shapes * len(steps),
        in_specs=[SMALL, WHOLE, DISTANT, DISTANT],
        out_specs=[WHOLE] * (len(pieces) * len(steps)),
        scratch_shapes=[
            pltpu.VMEM((2,) + own.shape[1:], jnp.bfloat16),
            pltpu.SemaphoreType.DMA((2,)),
        ],
        compiler_params=LIMIT,
        cost_estimate=pl.CostEstimate(
            flops=2 * rows * depth * parts * size * len(steps), bytes_accessed=4 * 2**20, transcendentals=0
        ),
    )(place, tokens, own, other)


def add_kernel(begin, first, second, out):
    rows = second.shape[0]
    total = first[begin : begin + rows].astype(jnp.float32) + second[...].astype(jnp.float32)
    out[begin : begin + rows] = total.astype(out.dtype)
    for low, high in ((0, begin), (begin + rows, out.shape[0])):
        if high > low:
            out[low:high] = first[low:high]


def added(first, second, begin=0):
    return pl.pallas_call(
        lambda *refs: add_kernel(begin, *refs),
        out_shape=jax.ShapeDtypeStruct(first.shape, first.dtype),
        in_specs=[WHOLE, WHOLE],
        out_specs=WHOLE,
        compiler_params=LIMIT,
        cost_estimate=pl.CostEstimate(flops=first.size, bytes_accessed=3 * 2**19, transcendentals=0),
    )(first, second)


def head_kernel(place, first, second, third, gains, theirs, query, pair):
    size = query.shape[1]
    heads = gains.shape[0] // 2
    owned = jnp.minimum(place[0], 2 * heads - 1)
    lane = jnp.where(owned >= heads, 1, 0)
    index = owned - lane * heads
    mine = lane == place[1]
    gain = []
    for part in range(2):
        at = pl.ds(part * heads + index, 1)
        gain.append(jnp.where(mine, gains[at], theirs[at]))
    total = first[...].astype(jnp.float32) + second[...].astype(jnp.float32)
    total = total + third[...].astype(jnp.float32)
    query[...] = head_norm(total[:, :size], gain[0]).astype(query.dtype)
    pair[:, :size] = head_norm(total[:, size : 2 * size], gain[1]).astype(pair.dtype)
    pair[:, size:] = total[:, 2 * size :].astype(pair.dtype)


def headed(place, first, second, third, gains, theirs):
    rows, size = first.shape[0], gains.shape[1]
    return pl.pallas_call(
        head_kernel,
        out_shape=[
            jax.ShapeDtypeStruct((rows, size), jnp.bfloat16),
            jax.ShapeDtypeStruct((rows, 2 * size), jnp.bfloat16),
        ],
        in_specs=[SMALL] + [WHOLE] * 5,
        out_specs=[WHOLE] * 2,
        compiler_params=LIMIT,
        cost_estimate=pl.CostEstimate(flops=10 * first.size, bytes_accessed=4 * 2**19, transcendentals=0),
    )(place, first, second, third, gains, theirs)


def attention_kernel(tok_rows, place, sliced, query, near, far, out, mixed):
    rows, size = query.shape
    blks = sliced.shape[0]
    chips = rows // (blks * tok_rows)
    key = lax.broadcasted_iota(jnp.int32, (1, rows), 1)
    chip = sum((key >= i * blks * tok_rows).astype(jnp.int32) for i in range(1, chips))
    rest = key - chip * (blks * tok_rows)
    blk = sum((rest >= i * tok_rows).astype(jnp.int32) for i in range(1, blks))
    begin = chip * (2 * tok_rows) + rest - blk * tok_rows
    limit = jnp.zeros((1, rows), jnp.float32)
    for i in range(blks):
        count = sliced[i, -2:, -1:][:1].astype(jnp.float32)
        limit = jnp.where(blk == i, count, limit)
    lanes = (place[1], 1 - place[1])
    valid = [(begin + lane * tok_rows).astype(jnp.float32) < limit for lane in lanes]
    pairs = (near, far)
    scores = []
    for pair, mask in zip(pairs, valid):
        product = lax.dot_general(
            query[...], pair[:, :size], (((1,), (1,)), ((), ())), preferred_element_type=jnp.float32
        )
        scores.append(jnp.where(mask, product * (size**-0.5), -1e30))
    top = jnp.maximum(*(jnp.max(score, axis=-1, keepdims=True) for score in scores))
    denom, total = 0.0, 0.0
    for score, pair in zip(scores, pairs):
        expo = jnp.exp(score - top)
        denom += jnp.sum(expo, axis=-1, keepdims=True)
        total += jnp.dot(expo.astype(jnp.bfloat16), pair[:, size:], preferred_element_type=jnp.float32)
    mixed[...] = total / denom
    for i in range(chips):
        for j in range(blks):
            begin = (i * blks + j) * tok_rows
            out[j * chips + i] = mixed[begin : begin + tok_rows].astype(out.dtype)


def attended(tok_rows, place, sliced, query, near, far):
    rows, size = query.shape
    return pl.pallas_call(
        lambda *refs: attention_kernel(tok_rows, *refs),
        out_shape=jax.ShapeDtypeStruct((rows // tok_rows, tok_rows, size), jnp.bfloat16),
        in_specs=[SMALL] + [WHOLE] * 4,
        out_specs=WHOLE,
        scratch_shapes=[pltpu.VMEM((rows, size), jnp.float32)],
        compiler_params=LIMIT,
        cost_estimate=pl.CostEstimate(
            flops=8 * rows * rows * size, bytes_accessed=2**20, transcendentals=2 * rows * rows
        ),
    )(place, sliced, query, near, far)


def merge_kernel(blocks, out):
    blks, chips = blocks.shape[:2]
    size = blocks.shape[3]
    heads = out.shape[2] // (chips * size)
    for chip in range(chips):
        for blk in range(heads):
            begin = (chip * heads + blk) * size
            out[0, :, begin : begin + size] = blocks[blk, chip]


def merged(blocks, shape):
    return pl.pallas_call(
        merge_kernel,
        out_shape=jax.ShapeDtypeStruct(shape, blocks.dtype),
        in_specs=[WHOLE],
        out_specs=WHOLE,
        compiler_params=LIMIT,
        cost_estimate=pl.CostEstimate(flops=0, bytes_accessed=2**19, transcendentals=0),
    )(blocks)


def on_device(stale, layer_of_section, mod_table, w_qkv, q_gain, k_gain, counts):
    tok_rows, width = stale.shape[1:]
    blks = lax.axis_size("blk")
    chips = lax.axis_size("zlo") * lax.axis_size("x")
    slice_width, head_size = w_qkv.shape[1], w_qkv.shape[4]

    received = shifted(dense(stale, (blks, 8, slice_width * 4 // 3)), "section", 1)
    modul = lax.dynamic_index_in_dim(mod_table, layer_of_section[0], 0, keepdims=False)
    place = jnp.stack([lax.axis_index("blk"), lax.axis_index("core")]).astype(jnp.int32)

    own = w_qkv[0].transpose(1, 2, 0, 3)
    gains = stacked(q_gain.transpose(1, 0, 2), k_gain.transpose(1, 0, 2))
    other = shifted(own, "core", 1)
    theirs = shifted(gains, "core", 1)

    sent = normed(counts, place, received, modul)
    sliced = lax.all_to_all(sent, "blk", 0, 0, tiled=False)
    copies = spread(sliced, other, (chips, blks * tok_rows, slice_width))
    tokens = lax.all_to_all(copies, CHIPS, 0, 0, tiled=False)
    tokens = tokens.reshape(chips * blks * tok_rows, slice_width)
    rows = tokens.shape[0]
    cut = rows // 4

    owners = 2 * own.shape[0]
    up, down = products((4,), place, tokens, own, other, (cut, rows - cut))
    up, down = passed(up, 1, 4, owners), passed(down, -1, 4, owners)
    three, five = products((3, 5), place, tokens, own, other)
    up, down = passed(added(three, up), 1, 3, owners), passed(added(five, down, cut), -1, 3, owners)
    two, six, one, seven, zero = products((2, 6, 1, 7, 0), place, tokens, own, other)
    up, down = passed(added(two, up), 1, 2, owners), passed(added(six, down), -1, 2, owners)
    up, down = passed(added(one, up), 1, 1, owners), passed(added(seven, down), -1, 1, owners)
    query, near = headed(place, zero, up, down, gains, theirs)
    far = shifted(near, "core", 1)

    mixed = attended(tok_rows, place, sliced, query, near, far)
    returned = lax.all_to_all(mixed, ("blk",) + CHIPS, 0, 0, tiled=False)
    return merged(returned.reshape(blks, chips, tok_rows, head_size), (1, tok_rows, width))


def solution(mesh):
    sizes = mesh.shape
    fine = Mesh(mesh.devices.reshape(sizes["section"], sizes["blk"], 2, 4, 2), AXES)
    uly = CHIPS + ("core",)
    in_specs = (
        P("section", ("blk",) + uly, None),
        P("section"),
        P(),
        P("section", "blk", uly, None, None),
        P("section", uly, None),
        P("section", uly, None),
        P("blk"),
    )
    out_specs = P("section", ("blk",) + uly, None)
    return jax.shard_map(
        on_device, mesh=fine, in_specs=in_specs, out_specs=out_specs, check_vma=False
    )
```

```python
import jax
import jax.numpy as jnp
from jax import lax
from jax.experimental import pallas as pl
from jax.experimental.pallas import tpu as pltpu
from jax.sharding import Mesh
from jax.sharding import PartitionSpec as P

AXES = ("section", "blk", "zlo", "x", "core")
CHIPS = ("zlo", "x")
SMALL = pl.BlockSpec(memory_space=pltpu.SMEM)
WHOLE = pl.BlockSpec(memory_space=pltpu.VMEM)
DISTANT = pl.BlockSpec(memory_space=pltpu.HBM)
LIMIT = pltpu.CompilerParams(vmem_limit_bytes=12 * 2**20)


def shifted(value, axis, steps):
    count = lax.axis_size(axis)
    pairs = [(source, (source + steps) % count) for source in range(count)]
    return lax.ppermute(value, axis, pairs)


def owns(row, blks):
    return (row + 1) % (blks // 2) != 0


def head_at(row, blks, heads):
    return jnp.minimum(jnp.where(row >= blks // 2, row - 1, row), heads - 1)


def passed(value, steps, ahead):
    blks = lax.axis_size("blk")
    pairs = [
        (row, (row + steps) % blks) for row in range(blks) if owns((row + steps * ahead) % blks, blks)
    ]
    return lax.ppermute(value, "blk", pairs)


def head_norm(values, gain):
    return values * lax.rsqrt(jnp.mean(values * values, axis=-1, keepdims=True) + 1e-06) * gain


def stack_kernel(q_gain, k_gain, gains):
    heads = q_gain.shape[0]
    for head in range(heads):
        gains[head : head + 1] = q_gain[head]
        gains[heads + head : heads + head + 1] = k_gain[head]


def stacked(q_gain, k_gain):
    return pl.pallas_call(
        stack_kernel,
        out_shape=jax.ShapeDtypeStruct((2 * q_gain.shape[0], q_gain.shape[2]), jnp.float32),
        in_specs=[WHOLE, WHOLE],
        out_specs=WHOLE,
        compiler_params=LIMIT,
        cost_estimate=pl.CostEstimate(flops=0, bytes_accessed=2**14, transcendentals=0),
    )(q_gain, k_gain)


def dense_kernel(stale, out, buffer):
    depth = out.shape[2] * 3 // 4
    piece = depth // 3
    for blk in range(out.shape[0]):
        block = stale[0, :, blk * depth : (blk + 1) * depth].astype(jnp.float32)
        buffer[blk, :, :depth] = block[:8]
        buffer[blk, 6:, depth:] = jnp.zeros((2, piece), jnp.float32)
        for token in range(2):
            for part in range(3):
                at = 3 * token + part
                buffer[blk, at : at + 1, depth:] = block[
                    8 + token : 9 + token, part * piece : (part + 1) * piece
                ]
    out[...] = buffer[...].astype(out.dtype)


def dense(stale, shape):
    return pl.pallas_call(
        dense_kernel,
        out_shape=jax.ShapeDtypeStruct(shape, jnp.bfloat16),
        in_specs=[WHOLE],
        out_specs=WHOLE,
        scratch_shapes=[pltpu.VMEM(shape, jnp.float32)],
        compiler_params=LIMIT,
        cost_estimate=pl.CostEstimate(flops=10**6, bytes_accessed=10**6, transcendentals=0),
    )(stale)


def norm_kernel(counts, place, stale, modul, out):
    blks, _, lanes = stale.shape
    depth = lanes * 3 // 4
    piece = depth // 3
    width = blks * depth
    source = stale[...].astype(jnp.float32)
    square = jnp.sum(source * source, axis=0)
    row = lax.broadcasted_iota(jnp.int32, (8, 1), 0)
    first = jnp.sum(square[:, :depth], axis=-1, keepdims=True)
    rest = jnp.sum(square[:, depth:], axis=-1, keepdims=True)
    eighth = jnp.sum(jnp.where(row < 3, rest, 0.0), axis=0, keepdims=True)
    ninth = jnp.sum(jnp.where((row >= 3) & (row < 6), rest, 0.0), axis=0, keepdims=True)
    spread = jnp.sqrt(first / width + 1e-06)
    last = jnp.sqrt(jnp.where(row < 3, eighth, ninth) / width + 1e-06)
    part = jnp.where(row < 3, row, row - 3)
    count = jnp.full((8, piece), counts[0], jnp.int32).astype(jnp.float32)
    for blk in range(blks):
        begin = blk * depth
        shift, scale = (modul[i : i + 1, begin : begin + depth] for i in (0, 1))
        normed = source[blk, :, :depth] / spread * (1.0 + scale) + shift
        out[blk, :, :depth] = normed.astype(out.dtype)
        shift, scale = (
            jnp.where(
                part == 0,
                values[:, :piece],
                jnp.where(part == 1, values[:, piece : 2 * piece], values[:, 2 * piece :]),
            )
            for values in (shift, scale)
        )
        normed = source[blk, :, depth:] / last * (1.0 + scale) + shift
        out[blk, :, depth:] = jnp.where(row < 6, normed, count).astype(out.dtype)


def normed(counts, place, stale, modul):
    return pl.pallas_call(
        norm_kernel,
        out_shape=jax.ShapeDtypeStruct(stale.shape, jnp.bfloat16),
        in_specs=[SMALL, SMALL, WHOLE, WHOLE],
        out_specs=WHOLE,
        compiler_params=LIMIT,
        cost_estimate=pl.CostEstimate(flops=10**10, bytes_accessed=10**6, transcendentals=0),
    )(counts, place, stale, modul)


def spread_kernel(sliced, weights, out, rows):
    blks, _, lanes = sliced.shape
    depth = lanes * 3 // 4
    piece = depth // 3
    tok_rows = rows.shape[0] // blks
    for blk in range(blks):
        block = sliced[blk].astype(jnp.float32)
        begin = blk * tok_rows
        rows[begin : begin + 8] = block[:, :depth]
        for token in range(2):
            for part in range(3):
                at = 3 * token + part
                rows[begin + 8 + token : begin + 9 + token, part * piece : (part + 1) * piece] = block[
                    at : at + 1, depth:
                ]
    block = rows[...].astype(out.dtype)
    for chip in range(out.shape[0]):
        out[chip] = block


def spread(sliced, weights, shape):
    return pl.pallas_call(
        spread_kernel,
        out_shape=jax.ShapeDtypeStruct(shape, jnp.bfloat16),
        in_specs=[WHOLE, DISTANT],
        out_specs=WHOLE,
        scratch_shapes=[pltpu.VMEM(shape[1:], jnp.float32)],
        compiler_params=LIMIT,
        cost_estimate=pl.CostEstimate(flops=0, bytes_accessed=10**6, transcendentals=0),
    )(sliced, weights)


def product_kernel(steps, place, tokens, own, other, *refs):
    outs, block, sems = refs[:-2], refs[-2], refs[-1]
    pieces = len(outs) // len(steps)
    row, core = place[0], place[1]
    heads, parts = own.shape[:2]

    def fetch(number):
        blks = lax.axis_size("blk")
        head = head_at(lax.rem(row + steps[number], blks), blks, 2 * heads)
        lane = jnp.where(head >= heads, 1, 0)
        slot = number % 2

        @pl.when(lane == core)
        def _():
            pltpu.make_async_copy(own.at[head - lane * heads], block.at[slot], sems.at[slot]).start()

        @pl.when(lane != core)
        def _():
            pltpu.make_async_copy(other.at[head - lane * heads], block.at[slot], sems.at[slot]).start()

    fetch(0)
    for number in range(len(steps)):
        slot = number % 2
        if number + 1 < len(steps):
            fetch(number + 1)
        pltpu.make_async_copy(own.at[0], block.at[slot], sems.at[slot]).wait()
        weights = jnp.concatenate([block[slot, part] for part in range(parts)], axis=1)
        total = jnp.dot(tokens[...], weights, preferred_element_type=jnp.float32)
        begin = 0
        for out in outs[number * pieces : (number + 1) * pieces]:
            out[...] = total[begin : begin + out.shape[0]].astype(out.dtype)
            begin += out.shape[0]


def products(steps, place, tokens, own, other, pieces=None):
    rows, depth = tokens.shape
    parts, size = own.shape[1], own.shape[3]
    pieces = pieces or (rows,)
    shapes = [jax.ShapeDtypeStruct((piece, parts * size), jnp.bfloat16) for piece in pieces]
    return pl.pallas_call(
        lambda *refs: product_kernel(steps, *refs),
        out_shape=shapes * len(steps),
        in_specs=[SMALL, WHOLE, DISTANT, DISTANT],
        out_specs=[WHOLE] * (len(pieces) * len(steps)),
        scratch_shapes=[
            pltpu.VMEM((2,) + own.shape[1:], jnp.bfloat16),
            pltpu.SemaphoreType.DMA((2,)),
        ],
        compiler_params=LIMIT,
        cost_estimate=pl.CostEstimate(
            flops=2 * rows * depth * parts * size * len(steps), bytes_accessed=4 * 2**20, transcendentals=0
        ),
    )(place, tokens, own, other)


def add_kernel(begin, first, second, out):
    rows = second.shape[0]
    total = first[begin : begin + rows].astype(jnp.float32) + second[...].astype(jnp.float32)
    out[begin : begin + rows] = total.astype(out.dtype)
    for low, high in ((0, begin), (begin + rows, out.shape[0])):
        if high > low:
            out[low:high] = first[low:high]


def added(first, second, begin=0):
    return pl.pallas_call(
        lambda *refs: add_kernel(begin, *refs),
        out_shape=jax.ShapeDtypeStruct(first.shape, first.dtype),
        in_specs=[WHOLE, WHOLE],
        out_specs=WHOLE,
        compiler_params=LIMIT,
        cost_estimate=pl.CostEstimate(flops=first.size, bytes_accessed=3 * 2**19, transcendentals=0),
    )(first, second)


def head_gain(place, gains, theirs, part):
    heads = gains.shape[0] // 2
    owned = head_at(place[0], lax.axis_size("blk"), 2 * heads)
    lane = jnp.where(owned >= heads, 1, 0)
    at = pl.ds(part * heads + owned - lane * heads, 1)
    return jnp.where(lane == place[1], gains[at], theirs[at])


def summed(refs, begin, end):
    return sum(ref[:, begin:end].astype(jnp.float32) for ref in refs)


def pair_kernel(place, first, second, third, gains, theirs, pair):
    size = pair.shape[1] // 2
    refs = (first, second, third)
    keys = head_norm(summed(refs, size, 2 * size), head_gain(place, gains, theirs, 1))
    pair[:, :size] = keys.astype(pair.dtype)
    pair[:, size:] = summed(refs, 2 * size, 3 * size).astype(pair.dtype)


def paired(place, first, second, third, gains, theirs):
    rows, size = first.shape[0], gains.shape[1]
    return pl.pallas_call(
        pair_kernel,
        out_shape=jax.ShapeDtypeStruct((rows, 2 * size), jnp.bfloat16),
        in_specs=[SMALL] + [WHOLE] * 5,
        out_specs=WHOLE,
        compiler_params=LIMIT,
        cost_estimate=pl.CostEstimate(flops=10 * first.size, bytes_accessed=4 * 2**19, transcendentals=0),
    )(place, first, second, third, gains, theirs)


def query_kernel(place, first, second, third, gains, theirs, query):
    size = query.shape[1]
    total = summed((first, second, third), 0, size)
    query[...] = head_norm(total, head_gain(place, gains, theirs, 0)).astype(query.dtype)


def queried(place, first, second, third, gains, theirs):
    rows, size = first.shape[0], gains.shape[1]
    return pl.pallas_call(
        query_kernel,
        out_shape=jax.ShapeDtypeStruct((rows, size), jnp.bfloat16),
        in_specs=[SMALL] + [WHOLE] * 5,
        out_specs=WHOLE,
        compiler_params=LIMIT,
        cost_estimate=pl.CostEstimate(flops=5 * first.size, bytes_accessed=2 * 2**19, transcendentals=0),
    )(place, first, second, third, gains, theirs)


def attention_kernel(tok_rows, place, sliced, query, near, far, out, mixed):
    rows, size = query.shape
    blks = sliced.shape[0]
    chips = rows // (blks * tok_rows)
    key = lax.broadcasted_iota(jnp.int32, (1, rows), 1)
    chip = sum((key >= i * blks * tok_rows).astype(jnp.int32) for i in range(1, chips))
    rest = key - chip * (blks * tok_rows)
    blk = sum((rest >= i * tok_rows).astype(jnp.int32) for i in range(1, blks))
    begin = chip * (2 * tok_rows) + rest - blk * tok_rows
    limit = jnp.zeros((1, rows), jnp.float32)
    for i in range(blks):
        count = sliced[i, -2:, -1:][:1].astype(jnp.float32)
        limit = jnp.where(blk == i, count, limit)
    lanes = (place[1], 1 - place[1])
    valid = [(begin + lane * tok_rows).astype(jnp.float32) < limit for lane in lanes]
    pairs = (near, far)
    scores = []
    for pair, mask in zip(pairs, valid):
        product = lax.dot_general(
            query[...], pair[:, :size], (((1,), (1,)), ((), ())), preferred_element_type=jnp.float32
        )
        scores.append(jnp.where(mask, product * (size**-0.5), -1e30))
    top = jnp.maximum(*(jnp.max(score, axis=-1, keepdims=True) for score in scores))
    denom, total = 0.0, 0.0
    for score, pair in zip(scores, pairs):
        expo = jnp.exp(score - top)
        denom += jnp.sum(expo, axis=-1, keepdims=True)
        total += jnp.dot(expo.astype(jnp.bfloat16), pair[:, size:], preferred_element_type=jnp.float32)
    mixed[...] = total / denom
    for i in range(chips):
        for j in range(blks):
            begin = (i * blks + j) * tok_rows
            out[j * chips + i] = mixed[begin : begin + tok_rows].astype(out.dtype)


def attended(tok_rows, place, sliced, query, near, far):
    rows, size = query.shape
    return pl.pallas_call(
        lambda *refs: attention_kernel(tok_rows, *refs),
        out_shape=jax.ShapeDtypeStruct((rows // tok_rows, tok_rows, size), jnp.bfloat16),
        in_specs=[SMALL] + [WHOLE] * 4,
        out_specs=WHOLE,
        scratch_shapes=[pltpu.VMEM((rows, size), jnp.float32)],
        compiler_params=LIMIT,
        cost_estimate=pl.CostEstimate(
            flops=8 * rows * rows * size, bytes_accessed=2**20, transcendentals=2 * rows * rows
        ),
    )(place, sliced, query, near, far)


def merge_kernel(blocks, out):
    blks, chips = blocks.shape[:2]
    size = blocks.shape[3]
    begin = 0
    for chip in range(chips):
        for blk in range(blks):
            if owns(blk, blks):
                out[0, :, begin : begin + size] = blocks[blk, chip]
                begin += size


def merged(blocks, shape):
    return pl.pallas_call(
        merge_kernel,
        out_shape=jax.ShapeDtypeStruct(shape, blocks.dtype),
        in_specs=[WHOLE],
        out_specs=WHOLE,
        compiler_params=LIMIT,
        cost_estimate=pl.CostEstimate(flops=0, bytes_accessed=2**19, transcendentals=0),
    )(blocks)


def on_device(stale, layer_of_section, mod_table, w_qkv, q_gain, k_gain, counts):
    tok_rows, width = stale.shape[1:]
    blks = lax.axis_size("blk")
    chips = lax.axis_size("zlo") * lax.axis_size("x")
    slice_width, head_size = w_qkv.shape[1], w_qkv.shape[4]

    received = shifted(dense(stale, (blks, 8, slice_width * 4 // 3)), "section", 1)
    modul = lax.dynamic_index_in_dim(mod_table, layer_of_section[0], 0, keepdims=False)
    place = jnp.stack([lax.axis_index("blk"), lax.axis_index("core")]).astype(jnp.int32)

    own = w_qkv[0].transpose(1, 2, 0, 3)
    gains = stacked(q_gain.transpose(1, 0, 2), k_gain.transpose(1, 0, 2))
    other = shifted(own, "core", 1)
    theirs = shifted(gains, "core", 1)

    sent = normed(counts, place, received, modul)
    sliced = lax.all_to_all(sent, "blk", 0, 0, tiled=False)
    copies = spread(sliced, other, (chips, blks * tok_rows, slice_width))
    tokens = lax.all_to_all(copies, CHIPS, 0, 0, tiled=False)
    tokens = tokens.reshape(chips * blks * tok_rows, slice_width)
    rows = tokens.shape[0]
    cut = rows // 4

    up, down = products((4,), place, tokens, own, other, (cut, rows - cut))
    up, down = passed(up, 1, 4), passed(down, -1, 4)
    three, five = products((3, 5), place, tokens, own, other)
    up, down = passed(added(three, up), 1, 3), passed(added(five, down, cut), -1, 3)
    two, six, one, seven, zero = products((2, 6, 1, 7, 0), place, tokens, own, other)
    up, down = passed(added(two, up), 1, 2), passed(added(six, down), -1, 2)
    up, down = passed(added(one, up), 1, 1), passed(added(seven, down), -1, 1)
    near = paired(place, zero, up, down, gains, theirs)
    far = shifted(near, "core", 1)
    query = queried(place, zero, up, down, gains, theirs)

    mixed = attended(tok_rows, place, sliced, query, near, far)
    returned = lax.all_to_all(mixed, ("blk",) + CHIPS, 0, 0, tiled=False)
    return merged(returned.reshape(blks, chips, tok_rows, head_size), (1, tok_rows, width))


def solution(mesh):
    sizes = mesh.shape
    fine = Mesh(mesh.devices.reshape(sizes["section"], sizes["blk"], 2, 4, 2), AXES)
    uly = CHIPS + ("core",)
    in_specs = (
        P("section", ("blk",) + uly, None),
        P("section"),
        P(),
        P("section", "blk", uly, None, None),
        P("section", uly, None),
        P("section", uly, None),
        P("blk"),
    )
    out_specs = P("section", ("blk",) + uly, None)
    return jax.shard_map(
        on_device, mesh=fine, in_specs=in_specs, out_specs=out_specs, check_vma=False
    )
```

```python
import jax
import jax.numpy as jnp
from jax import lax
from jax.experimental import pallas as pl
from jax.experimental.pallas import tpu as pltpu
from jax.sharding import Mesh
from jax.sharding import PartitionSpec as P

AXES = ("section", "blk", "zlo", "x", "core")
CHIPS = ("zlo", "x")
SMALL = pl.BlockSpec(memory_space=pltpu.SMEM)
WHOLE = pl.BlockSpec(memory_space=pltpu.VMEM)
DISTANT = pl.BlockSpec(memory_space=pltpu.HBM)
LIMIT = pltpu.CompilerParams(vmem_limit_bytes=12 * 2**20)


def shifted(value, axis, steps):
    count = lax.axis_size(axis)
    pairs = [(source, (source + steps) % count) for source in range(count)]
    return lax.ppermute(value, axis, pairs)


def owns(row, blks):
    return (row + 1) % (blks // 2) != 0


def head_at(row, blks, heads):
    return jnp.minimum(jnp.where(row >= blks // 2, row - 1, row), heads - 1)


def passed(value, steps, ahead):
    blks = lax.axis_size("blk")
    pairs = [
        (row, (row + steps) % blks) for row in range(blks) if owns((row + steps * ahead) % blks, blks)
    ]
    return lax.ppermute(value, "blk", pairs)


def head_norm(values, gain):
    return values * lax.rsqrt(jnp.mean(values * values, axis=-1, keepdims=True) + 1e-06) * gain


def stack_kernel(q_gain, k_gain, gains):
    heads = q_gain.shape[0]
    for head in range(heads):
        gains[head : head + 1] = q_gain[head]
        gains[heads + head : heads + head + 1] = k_gain[head]


def stacked(q_gain, k_gain):
    return pl.pallas_call(
        stack_kernel,
        out_shape=jax.ShapeDtypeStruct((2 * q_gain.shape[0], q_gain.shape[2]), jnp.float32),
        in_specs=[WHOLE, WHOLE],
        out_specs=WHOLE,
        compiler_params=LIMIT,
        cost_estimate=pl.CostEstimate(flops=0, bytes_accessed=2**14, transcendentals=0),
    )(q_gain, k_gain)


def dense_kernel(stale, out, buffer):
    depth = out.shape[2] * 3 // 4
    piece = depth // 3
    for blk in range(out.shape[0]):
        block = stale[0, :, blk * depth : (blk + 1) * depth].astype(jnp.float32)
        buffer[blk, :, :depth] = block[:8]
        buffer[blk, 6:, depth:] = jnp.zeros((2, piece), jnp.float32)
        for token in range(2):
            for part in range(3):
                at = 3 * token + part
                buffer[blk, at : at + 1, depth:] = block[
                    8 + token : 9 + token, part * piece : (part + 1) * piece
                ]
    out[...] = buffer[...].astype(out.dtype)


def dense(stale, shape):
    return pl.pallas_call(
        dense_kernel,
        out_shape=jax.ShapeDtypeStruct(shape, jnp.bfloat16),
        in_specs=[WHOLE],
        out_specs=WHOLE,
        scratch_shapes=[pltpu.VMEM(shape, jnp.float32)],
        compiler_params=LIMIT,
        cost_estimate=pl.CostEstimate(flops=10**6, bytes_accessed=10**6, transcendentals=0),
    )(stale)


def norm_kernel(counts, place, stale, modul, out):
    blks, _, lanes = stale.shape
    depth = lanes * 3 // 4
    piece = depth // 3
    width = blks * depth
    source = stale[...].astype(jnp.float32)
    square = jnp.sum(source * source, axis=0)
    row = lax.broadcasted_iota(jnp.int32, (8, 1), 0)
    first = jnp.sum(square[:, :depth], axis=-1, keepdims=True)
    rest = jnp.sum(square[:, depth:], axis=-1, keepdims=True)
    eighth = jnp.sum(jnp.where(row < 3, rest, 0.0), axis=0, keepdims=True)
    ninth = jnp.sum(jnp.where((row >= 3) & (row < 6), rest, 0.0), axis=0, keepdims=True)
    spread = jnp.sqrt(first / width + 1e-06)
    last = jnp.sqrt(jnp.where(row < 3, eighth, ninth) / width + 1e-06)
    part = jnp.where(row < 3, row, row - 3)
    count = jnp.full((8, piece), counts[0], jnp.int32).astype(jnp.float32)
    for blk in range(blks):
        begin = blk * depth
        shift, scale = (modul[i : i + 1, begin : begin + depth] for i in (0, 1))
        normed = source[blk, :, :depth] / spread * (1.0 + scale) + shift
        out[blk, :, :depth] = normed.astype(out.dtype)
        shift, scale = (
            jnp.where(
                part == 0,
                values[:, :piece],
                jnp.where(part == 1, values[:, piece : 2 * piece], values[:, 2 * piece :]),
            )
            for values in (shift, scale)
        )
        normed = source[blk, :, depth:] / last * (1.0 + scale) + shift
        out[blk, :, depth:] = jnp.where(row < 6, normed, count).astype(out.dtype)


def normed(counts, place, stale, modul):
    return pl.pallas_call(
        norm_kernel,
        out_shape=jax.ShapeDtypeStruct(stale.shape, jnp.bfloat16),
        in_specs=[SMALL, SMALL, WHOLE, WHOLE],
        out_specs=WHOLE,
        compiler_params=LIMIT,
        cost_estimate=pl.CostEstimate(flops=10**10, bytes_accessed=10**6, transcendentals=0),
    )(counts, place, stale, modul)


def spread_kernel(sliced, weights, out, rows):
    blks, _, lanes = sliced.shape
    depth = lanes * 3 // 4
    piece = depth // 3
    tok_rows = rows.shape[0] // blks
    for blk in range(blks):
        block = sliced[blk].astype(jnp.float32)
        begin = blk * tok_rows
        rows[begin : begin + 8] = block[:, :depth]
        for token in range(2):
            for part in range(3):
                at = 3 * token + part
                rows[begin + 8 + token : begin + 9 + token, part * piece : (part + 1) * piece] = block[
                    at : at + 1, depth:
                ]
    block = rows[...].astype(out.dtype)
    for chip in range(out.shape[0]):
        out[chip] = block


def spread(sliced, weights, shape):
    return pl.pallas_call(
        spread_kernel,
        out_shape=jax.ShapeDtypeStruct(shape, jnp.bfloat16),
        in_specs=[WHOLE, DISTANT],
        out_specs=WHOLE,
        scratch_shapes=[pltpu.VMEM(shape[1:], jnp.float32)],
        compiler_params=LIMIT,
        cost_estimate=pl.CostEstimate(flops=0, bytes_accessed=10**6, transcendentals=0),
    )(sliced, weights)


def product_kernel(steps, place, tokens, own, other, *refs):
    outs, block, sems = refs[:-2], refs[-2], refs[-1]
    pieces = len(outs) // len(steps)
    row, core = place[0], place[1]
    heads, parts = own.shape[:2]

    def fetch(number):
        blks = lax.axis_size("blk")
        head = head_at(lax.rem(row + steps[number], blks), blks, 2 * heads)
        lane = jnp.where(head >= heads, 1, 0)
        slot = number % 2

        @pl.when(lane == core)
        def _():
            pltpu.make_async_copy(own.at[head - lane * heads], block.at[slot], sems.at[slot]).start()

        @pl.when(lane != core)
        def _():
            pltpu.make_async_copy(other.at[head - lane * heads], block.at[slot], sems.at[slot]).start()

    fetch(0)
    for number in range(len(steps)):
        slot = number % 2
        if number + 1 < len(steps):
            fetch(number + 1)
        pltpu.make_async_copy(own.at[0], block.at[slot], sems.at[slot]).wait()
        weights = jnp.concatenate([block[slot, part] for part in range(parts)], axis=1)
        total = jnp.dot(tokens[...], weights, preferred_element_type=jnp.float32)
        begin = 0
        for out in outs[number * pieces : (number + 1) * pieces]:
            out[...] = total[begin : begin + out.shape[0]].astype(out.dtype)
            begin += out.shape[0]


def products(steps, place, tokens, own, other, pieces=None):
    rows, depth = tokens.shape
    parts, size = own.shape[1], own.shape[3]
    pieces = pieces or (rows,)
    shapes = [jax.ShapeDtypeStruct((piece, parts * size), jnp.bfloat16) for piece in pieces]
    return pl.pallas_call(
        lambda *refs: product_kernel(steps, *refs),
        out_shape=shapes * len(steps),
        in_specs=[SMALL, WHOLE, DISTANT, DISTANT],
        out_specs=[WHOLE] * (len(pieces) * len(steps)),
        scratch_shapes=[
            pltpu.VMEM((2,) + own.shape[1:], jnp.bfloat16),
            pltpu.SemaphoreType.DMA((2,)),
        ],
        compiler_params=LIMIT,
        cost_estimate=pl.CostEstimate(
            flops=2 * rows * depth * parts * size * len(steps), bytes_accessed=4 * 2**20, transcendentals=0
        ),
    )(place, tokens, own, other)


def add_kernel(begin, first, second, out):
    rows = second.shape[0]
    total = first[begin : begin + rows].astype(jnp.float32) + second[...].astype(jnp.float32)
    out[begin : begin + rows] = total.astype(out.dtype)
    for low, high in ((0, begin), (begin + rows, out.shape[0])):
        if high > low:
            out[low:high] = first[low:high]


def added(first, second, begin=0):
    return pl.pallas_call(
        lambda *refs: add_kernel(begin, *refs),
        out_shape=jax.ShapeDtypeStruct(first.shape, first.dtype),
        in_specs=[WHOLE, WHOLE],
        out_specs=WHOLE,
        compiler_params=LIMIT,
        cost_estimate=pl.CostEstimate(flops=first.size, bytes_accessed=3 * 2**19, transcendentals=0),
    )(first, second)


def head_gain(place, gains, theirs, part):
    heads = gains.shape[0] // 2
    owned = head_at(place[0], lax.axis_size("blk"), 2 * heads)
    lane = jnp.where(owned >= heads, 1, 0)
    at = pl.ds(part * heads + owned - lane * heads, 1)
    return jnp.where(lane == place[1], gains[at], theirs[at])


def summed(refs, begin, end):
    return sum(ref[:, begin:end].astype(jnp.float32) for ref in refs)


def pair_kernel(place, first, second, third, gains, theirs, pair):
    size = pair.shape[1] // 2
    refs = (first, second, third)
    keys = head_norm(summed(refs, size, 2 * size), head_gain(place, gains, theirs, 1))
    pair[:, :size] = keys.astype(pair.dtype)
    pair[:, size:] = summed(refs, 2 * size, 3 * size).astype(pair.dtype)


def paired(place, first, second, third, gains, theirs):
    rows, size = first.shape[0], gains.shape[1]
    return pl.pallas_call(
        pair_kernel,
        out_shape=jax.ShapeDtypeStruct((rows, 2 * size), jnp.bfloat16),
        in_specs=[SMALL] + [WHOLE] * 5,
        out_specs=WHOLE,
        compiler_params=LIMIT,
        cost_estimate=pl.CostEstimate(flops=10 * first.size, bytes_accessed=4 * 2**19, transcendentals=0),
    )(place, first, second, third, gains, theirs)


def query_kernel(place, first, second, third, gains, theirs, query):
    size = query.shape[1]
    total = summed((first, second, third), 0, size)
    query[...] = head_norm(total, head_gain(place, gains, theirs, 0)).astype(query.dtype)


def queried(place, first, second, third, gains, theirs):
    rows, size = first.shape[0], gains.shape[1]
    return pl.pallas_call(
        query_kernel,
        out_shape=jax.ShapeDtypeStruct((rows, size), jnp.bfloat16),
        in_specs=[SMALL] + [WHOLE] * 5,
        out_specs=WHOLE,
        compiler_params=LIMIT,
        cost_estimate=pl.CostEstimate(flops=5 * first.size, bytes_accessed=2 * 2**19, transcendentals=0),
    )(place, first, second, third, gains, theirs)


def attention_kernel(tok_rows, place, sliced, query, near, far, out, mixed):
    rows, size = query.shape
    blks = sliced.shape[0]
    chips = rows // (blks * tok_rows)
    key = lax.broadcasted_iota(jnp.int32, (1, rows), 1)
    chip = sum((key >= i * blks * tok_rows).astype(jnp.int32) for i in range(1, chips))
    rest = key - chip * (blks * tok_rows)
    blk = sum((rest >= i * tok_rows).astype(jnp.int32) for i in range(1, blks))
    begin = chip * (2 * tok_rows) + rest - blk * tok_rows
    limit = jnp.zeros((1, rows), jnp.float32)
    for i in range(blks):
        count = sliced[i, -2:, -1:][:1].astype(jnp.float32)
        limit = jnp.where(blk == i, count, limit)
    lanes = (place[1], 1 - place[1])
    valid = [(begin + lane * tok_rows).astype(jnp.float32) < limit for lane in lanes]
    pairs = (near, far)
    scores = []
    for pair, mask in zip(pairs, valid):
        product = lax.dot_general(
            query[...], pair[:, :size], (((1,), (1,)), ((), ())), preferred_element_type=jnp.float32
        )
        scores.append(jnp.where(mask, product * (size**-0.5), -1e30))
    top = jnp.maximum(*(jnp.max(score, axis=-1, keepdims=True) for score in scores))
    denom, total = 0.0, 0.0
    for score, pair in zip(scores, pairs):
        expo = jnp.exp(score - top)
        denom += jnp.sum(expo, axis=-1, keepdims=True)
        total += jnp.dot(expo.astype(jnp.bfloat16), pair[:, size:], preferred_element_type=jnp.float32)
    mixed[...] = total / denom
    for i in range(chips):
        for j in range(blks):
            begin = (i * blks + j) * tok_rows
            out[j * chips + i] = mixed[begin : begin + tok_rows].astype(out.dtype)


def attended(tok_rows, place, sliced, query, near, far):
    rows, size = query.shape
    return pl.pallas_call(
        lambda *refs: attention_kernel(tok_rows, *refs),
        out_shape=jax.ShapeDtypeStruct((rows // tok_rows, tok_rows, size), jnp.bfloat16),
        in_specs=[SMALL] + [WHOLE] * 4,
        out_specs=WHOLE,
        scratch_shapes=[pltpu.VMEM((rows, size), jnp.float32)],
        compiler_params=LIMIT,
        cost_estimate=pl.CostEstimate(
            flops=8 * rows * rows * size, bytes_accessed=2**20, transcendentals=2 * rows * rows
        ),
    )(place, sliced, query, near, far)


def merge_kernel(blocks, out):
    blks, chips = blocks.shape[:2]
    size = blocks.shape[3]
    begin = 0
    for chip in range(chips):
        for blk in range(blks):
            if owns(blk, blks):
                out[0, :, begin : begin + size] = blocks[blk, chip]
                begin += size


def merged(blocks, shape):
    return pl.pallas_call(
        merge_kernel,
        out_shape=jax.ShapeDtypeStruct(shape, blocks.dtype),
        in_specs=[WHOLE],
        out_specs=WHOLE,
        compiler_params=LIMIT,
        cost_estimate=pl.CostEstimate(flops=0, bytes_accessed=2**19, transcendentals=0),
    )(blocks)


def on_device(stale, layer_of_section, mod_table, w_qkv, q_gain, k_gain, counts):
    tok_rows, width = stale.shape[1:]
    blks = lax.axis_size("blk")
    chips = lax.axis_size("zlo") * lax.axis_size("x")
    slice_width, head_size = w_qkv.shape[1], w_qkv.shape[4]

    received = shifted(dense(stale, (blks, 8, slice_width * 4 // 3)), "section", 1)
    modul = lax.dynamic_index_in_dim(mod_table, layer_of_section[0], 0, keepdims=False)
    place = jnp.stack([lax.axis_index("blk"), lax.axis_index("core")]).astype(jnp.int32)

    own = w_qkv[0].transpose(1, 2, 0, 3)
    gains = stacked(q_gain.transpose(1, 0, 2), k_gain.transpose(1, 0, 2))
    other = shifted(own, "core", 1)
    theirs = shifted(gains, "core", 1)

    sent = normed(counts, place, received, modul)
    sliced = lax.all_to_all(sent, "blk", 0, 0, tiled=False)
    copies = spread(sliced, other, (chips, blks * tok_rows, slice_width))
    tokens = lax.all_to_all(copies, CHIPS, 0, 0, tiled=False)
    tokens = tokens.reshape(chips * blks * tok_rows, slice_width)
    rows = tokens.shape[0]
    cut = rows // 5

    up, down = products((4,), place, tokens, own, other, (cut, rows - cut))
    up, down = passed(up, 1, 4), passed(down, -1, 4)
    three, five = products((3, 5), place, tokens, own, other)
    up, down = passed(added(three, up), 1, 3), passed(added(five, down, cut), -1, 3)
    two, six, one, seven, zero = products((2, 6, 1, 7, 0), place, tokens, own, other)
    up, down = passed(added(two, up), 1, 2), passed(added(six, down), -1, 2)
    up, down = passed(added(one, up), 1, 1), passed(added(seven, down), -1, 1)
    near = paired(place, zero, up, down, gains, theirs)
    far = shifted(near, "core", 1)
    query = queried(place, zero, up, down, gains, theirs)

    mixed = attended(tok_rows, place, sliced, query, near, far)
    returned = lax.all_to_all(mixed, ("blk",) + CHIPS, 0, 0, tiled=False)
    return merged(returned.reshape(blks, chips, tok_rows, head_size), (1, tok_rows, width))


def solution(mesh):
    sizes = mesh.shape
    fine = Mesh(mesh.devices.reshape(sizes["section"], sizes["blk"], 2, 4, 2), AXES)
    uly = CHIPS + ("core",)
    in_specs = (
        P("section", ("blk",) + uly, None),
        P("section"),
        P(),
        P("section", "blk", uly, None, None),
        P("section", uly, None),
        P("section", uly, None),
        P("blk"),
    )
    out_specs = P("section", ("blk",) + uly, None)
    return jax.shard_map(
        on_device, mesh=fine, in_specs=in_specs, out_specs=out_specs, check_vma=False
    )
```
